32 devices in a mesh: dp: 4 (over z), seq: 4 (over y, x), tensor: 2 (over core).
Axes of the slice: x: 2, y: 2, z: 4, core: 2. Of those that a mesh axis runs over, the one named last changes fastest.
Arguments:
- clips_a: bfloat16 [8, 8, 256, 1024], P('dp', 'seq', 'tensor'), may hold values from -6 to 6
- actions_a: int32 [8, 8], P('dp', 'seq'), may hold values from 0 to 7
- clips_b: bfloat16 [8, 8, 64, 1024], P('dp', 'seq', 'tensor'), may hold values from -6 to 6
- actions_b: int32 [8, 8], P('dp', 'seq'), may hold values from 0 to 7
- space_in: bfloat16 [3, 1024, 1024], P(None, ('dp', 'seq'), 'tensor'), may hold values from -0.1875 to 0.1875
- space_out: bfloat16 [1024, 1024], P(('dp', 'seq'), 'tensor'), may hold values from -1.5 to 1.5
- time_in: bfloat16 [3, 1024, 1024], P(None, ('dp', 'seq'), 'tensor'), may hold values from -0.1875 to 0.1875
- time_out: bfloat16 [1024, 1024], P(('dp', 'seq'), 'tensor'), may hold values from -0.375 to 0.375
- ffn_up: bfloat16 [1024, 4096], P(('dp', 'seq'), 'tensor'), may hold values from -0.1875 to 0.1875
- ffn_down: bfloat16 [1024, 4096], P(('dp', 'seq'), 'tensor'), may hold values from -0.125 to 0.125
- norm_gain: bfloat16 [3, 1024], P(None, ('dp', 'seq', 'tensor')), may hold values from 0.5 to 1.5
- norm_shift: bfloat16 [3, 1024], P(None, ('dp', 'seq', 'tensor')), may hold values from -1.796875 to 1.796875
- action_table: bfloat16 [8, 1024], P(None, ('dp', 'seq', 'tensor')), may hold values from -3 to 3
- cot_a: bfloat16 [8, 8, 256, 1024], P('dp', 'seq', 'tensor'), may hold values from -6 to 6
- cot_b: bfloat16 [8, 8, 64, 1024], P('dp', 'seq', 'tensor'), may hold values from -6 to 6
Outputs:
- mixed_a: bfloat16 [8, 8, 256, 1024], P('dp', 'seq', 'tensor')
- mixed_b: bfloat16 [8, 8, 64, 1024], P('dp', 'seq', 'tensor')
- grad_a: bfloat16 [8, 8, 256, 1024], P('dp', 'seq', 'tensor')
- grad_b: bfloat16 [8, 8, 64, 1024], P('dp', 'seq', 'tensor')
- grad_space_in: float32 [3, 1024, 1024], P(None, ('dp', 'seq'), 'tensor')
- grad_space_out: float32 [1024, 1024], P(('dp', 'seq'), 'tensor')
- grad_time_in: float32 [3, 1024, 1024], P(None, ('dp', 'seq'), 'tensor')
- grad_time_out: float32 [1024, 1024], P(('dp', 'seq'), 'tensor')
- grad_ffn_up: float32 [1024, 4096], P(('dp', 'seq'), 'tensor')
- grad_ffn_down: float32 [1024, 4096], P(('dp', 'seq'), 'tensor')
- grad_gain: float32 [3, 1024], P(None, ('dp', 'seq', 'tensor'))
- grad_shift: float32 [3, 1024], P(None, ('dp', 'seq', 'tensor'))
- grad_table: float32 [8, 1024], P(None, ('dp', 'seq', 'tensor'))
The draws below stay inside these ranges and needn't reach their ends.
All inputs are finite; a program needn't handle non-finite values.
Results may differ from the reference program's by a relative error of at most 0.022.
Values may be sent and summed in bfloat16 or wider, within the bound.
No kernel may reach another device: no remote copies, remote signals or barrier semaphores. Data moves between devices by JAX's collectives and lax.ppermute only.
A program may use at most 192 MiB of HBM per device.

```python
import jax
import jax.numpy as jnp
from jax import lax

D = 1024
HEADS = 16
HDIM = 64
FF = 4096
ACTIONS = 8
P_A = 256
P_B = 64
FRAMES = 8
CLIPS_A = 8
CLIPS_B = 8


def with_ends(array, own_key, smallest, top_value):
    longest = array.shape.index(max(array.shape))
    spots = []
    for shift in (0, 1):
        where = [jax.random.randint(jax.random.fold_in(own_key, axis), (), 0, length) for axis, length in enumerate(array.shape)]
        where[longest] = (where[longest] + shift) % array.shape[longest]
        spots.append(tuple(where))
    return array.at[spots[0]].set(smallest).at[spots[1]].set(top_value)


def block_levels(own_key, shape, shards, least, top_value):
    level = 1.0
    for axis_at, shards_of in shards:
        heights = jax.random.uniform(jax.random.fold_in(jax.random.fold_in(own_key, 6), axis_at), (shards_of,), jnp.float32, least / len(shards), top_value / len(shards))
        level = level * jnp.repeat(jnp.exp(heights), shape[axis_at] // shards_of).reshape((-1,) + (1,) * (len(shape) - 1 - axis_at))
    return level


def normal_values(rng, shape, spread, limit, shards=(), kind=jnp.bfloat16):
    entries = spread * jax.random.normal(rng, shape, jnp.float32)
    if shards:
        entries = entries * block_levels(rng, shape, shards, -0.22, 0.18)
    return jnp.clip(entries, -limit, limit).astype(kind)


def setup_inputs(seed: int = 0) -> dict:
    key_of = jax.random.split(jax.random.key(seed), 16)
    clips_a = normal_values(key_of[0], (CLIPS_A, FRAMES, P_A, D), 1.0, 6.0, ((0, 4), (1, 4), (2, 2)))
    actions_a = with_ends(jax.random.randint(key_of[1], (CLIPS_A, FRAMES), 0, ACTIONS), jax.random.fold_in(key_of[1], 1), 0, ACTIONS - 1).astype(jnp.int32)
    clips_b = normal_values(key_of[2], (CLIPS_B, FRAMES, P_B, D), 1.0, 6.0, ((0, 4), (1, 4), (2, 2)))
    actions_b = with_ends(jax.random.randint(key_of[3], (CLIPS_B, FRAMES), 0, ACTIONS), jax.random.fold_in(key_of[3], 1), 0, ACTIONS - 1).astype(jnp.int32)
    space_in = normal_values(key_of[4], (3, D, D), D ** -0.5, 0.1875, ((1, 16), (2, 2)))
    space_out = normal_values(key_of[5], (D, D), 16 ** -0.5, 1.5, ((0, 16), (1, 2)))
    time_in = normal_values(key_of[6], (3, D, D), D ** -0.5, 0.1875, ((1, 16), (2, 2)))
    time_out = normal_values(key_of[7], (D, D), (D // 4) ** -0.5, 0.375, ((0, 16), (1, 2)))
    ffn_up = normal_values(key_of[8], (D, FF), D ** -0.5, 0.1875, ((0, 16), (1, 2)))
    ffn_down = normal_values(key_of[9], (D, FF), (FF // 2) ** -0.5, 0.125, ((0, 16), (1, 2)))
    norm_gain = jnp.clip(1.0 + 0.1 * jax.random.normal(key_of[10], (3, D), jnp.float32), 0.5, 1.5).astype(jnp.bfloat16)
    norm_shift = normal_values(key_of[11], (3, D), 0.3, 1.796875, ((1, 32),))
    action_table = normal_values(key_of[12], (ACTIONS, D), 0.5, 3.0, ((1, 32),))
    cot_a = normal_values(key_of[13], (CLIPS_A, FRAMES, P_A, D), 1.0, 6.0, ((0, 4), (1, 4), (2, 2)))
    cot_b = normal_values(key_of[14], (CLIPS_B, FRAMES, P_B, D), 1.0, 6.0, ((0, 4), (1, 4), (2, 2)))
    return {"clips_a": clips_a, "actions_a": actions_a, "clips_b": clips_b, "actions_b": actions_b, "space_in": space_in, "space_out": space_out, "time_in": time_in, "time_out": time_out, "ffn_up": ffn_up, "ffn_down": ffn_down, "norm_gain": norm_gain, "norm_shift": norm_shift, "action_table": action_table, "cot_a": cot_a, "cot_b": cot_b}


highest = lax.Precision.HIGHEST
epsilon = 1e-05
masked_score = -1e+30

@jax.custom_vjp
def low(v):
    return lax.optimization_barrier(v.astype(jnp.bfloat16)).astype(jnp.float32)

@jax.custom_vjp
def low_back(v):
    return v

def low_keep(v):
    return (low(v), None)

def low_pass(kept, grad):
    return (grad,)

def back_keep(v):
    return (v, None)

def back_low(kept, grad):
    return (low(grad),)
low.defvjp(low_keep, low_pass)
low_back.defvjp(back_keep, back_low)

def layer_norm(operand, gain_row, shift_row):
    centred = operand - lax.optimization_barrier(jnp.mean(operand, axis=-1, keepdims=True))
    inverse = lax.rsqrt(lax.optimization_barrier(jnp.mean(centred * centred, axis=-1, keepdims=True)) + epsilon)
    return centred * inverse * gain_row + shift_row

def attend(normed, w_in, w_out, causal):
    frames, places, features = normed.shape
    packed = jnp.einsum('fpd,sde->sfpe', normed, w_in, precision=highest)
    queries = low_back(low(packed[0])).reshape(frames, places, HEADS, HDIM)
    keys_all = low_back(low(packed[1])).reshape(frames, places, HEADS, HDIM)
    values_all = low_back(low(packed[2])).reshape(frames, places, HEADS, HDIM)
    scaling = HDIM ** (-0.5)
    if causal:
        scores = low_back(jnp.einsum('fphd,gphd->phfg', queries, keys_all, precision=highest) * scaling)
        allowed = jnp.arange(frames)[:, None] >= jnp.arange(frames)[None, :]
        scores = jnp.where(allowed, scores, masked_score)
    else:
        scores = low_back(jnp.einsum('fphd,fqhd->fhpq', queries, keys_all, precision=highest) * scaling)
    row_max = lax.optimization_barrier(jnp.max(scores, axis=-1, keepdims=True))
    shifted = jnp.exp(scores - row_max)
    attn_weights = low(shifted / lax.optimization_barrier(jnp.sum(shifted, axis=-1, keepdims=True)))
    if causal:
        mixed_out = jnp.einsum('phfg,gphd->fphd', attn_weights, values_all, precision=highest)
    else:
        mixed_out = jnp.einsum('fhpq,fqhd->fphd', attn_weights, values_all, precision=highest)
    mixed_out = low_back(low(mixed_out.reshape(frames, places, features)))
    return low_back(jnp.einsum('fpe,de->fpd', mixed_out, w_out, precision=highest))

def block(clip_data, onehot, params):
    space_in, space_out, time_in, time_out, ffn_up, ffn_down, norm_gain, norm_shift, action_table = params
    entered = clip_data + jnp.dot(onehot, action_table, precision=highest)[:, None, :]
    middle = entered + attend(low(layer_norm(entered, norm_gain[0], norm_shift[0])), space_in, space_out, False)
    before_ffn = middle + attend(low(layer_norm(middle, norm_gain[1], norm_shift[1])), time_in, time_out, True)
    normed = low(layer_norm(before_ffn, norm_gain[2], norm_shift[2]))
    upward = low_back(jnp.einsum('fpd,dh->fph', normed, ffn_up, precision=highest))
    active = low(jax.nn.gelu(upward))
    return before_ffn + low_back(jnp.einsum('fph,dh->fpd', active, ffn_down, precision=highest))

def reference(clips_a, actions_a, clips_b, actions_b, space_in, space_out, time_in, time_out, ffn_up, ffn_down, norm_gain, norm_shift, action_table, cot_a, cot_b):
    weights = tuple((tensor.astype(jnp.float32) for tensor in (space_in, space_out, time_in, time_out, ffn_up, ffn_down, norm_gain, norm_shift, action_table)))

    def run_batch(clips, actions, cotangent, totals_in):

        def one_clip(carry, scanned):
            clip_data, clip_actions, clip_cot = scanned
            onehot = (clip_actions[:, None] == jnp.arange(ACTIONS, dtype=jnp.int32)[None, :]).astype(jnp.float32)
            output, pullback = jax.vjp(lambda inputs, params: block(inputs, onehot, params), clip_data.astype(jnp.float32), weights)
            d_input, d_params = pullback(clip_cot.astype(jnp.float32))
            carry = tuple((left + right for left, right in zip(carry, d_params)))
            return (carry, (output.astype(jnp.bfloat16), d_input.astype(jnp.bfloat16)))
        return lax.scan(one_clip, totals_in, (clips, actions, cotangent))
    zeros_all = tuple((jnp.zeros_like(tensor) for tensor in weights))
    totals, (mixed_a, grad_a) = run_batch(clips_a, actions_a, cot_a, zeros_all)
    totals, (mixed_b, grad_b) = run_batch(clips_b, actions_b, cot_b, totals)
    return (mixed_a, mixed_b, grad_a, grad_b, totals[0], totals[1], totals[2], totals[3], totals[4], totals[5], totals[6], totals[7], totals[8])
```

```python
import functools

import jax
import jax.numpy as jnp
from jax import lax
from jax.experimental import pallas as pl
from jax.experimental.pallas import tpu as pltpu
from jax.sharding import PartitionSpec as P

HDIM = 64
BLOCK = 128

epsilon = 1e-05
masked_score = -1e30
highest = lax.Precision.HIGHEST
bf16 = jnp.bfloat16
f32 = jnp.float32


def swap(operand, axis, size, step):
    return lax.ppermute(operand, axis, [(i, i ^ step) for i in range(size)])


def norm_stats(operand):
    centred = operand - jnp.mean(operand, axis=-1, keepdims=True)
    inverse = lax.rsqrt(jnp.mean(centred * centred, axis=-1, keepdims=True) + epsilon)
    return centred * inverse, inverse


def layer_norm(operand, gain_row, shift_row):
    standard, _ = norm_stats(operand)
    return (standard * gain_row + shift_row).astype(bf16)


def norm_back(operand, gain_row, upstream):
    standard, inverse = norm_stats(operand)
    scaled = upstream * gain_row
    inner = (
        scaled
        - jnp.mean(scaled, axis=-1, keepdims=True)
        - standard * jnp.mean(scaled * standard, axis=-1, keepdims=True)
    )
    return inverse * inner, jnp.sum(upstream * standard, axis=0), jnp.sum(upstream, axis=0)


SLAB = 2 * HDIM


def nt(left, right):
    return lax.dot_general(left, right, (((1,), (1,)), ((), ())), preferred_element_type=f32)


def nn(left, right):
    return lax.dot_general(left, right, (((1,), (0,)), ((), ())), preferred_element_type=f32)


def tn(left, right):
    return lax.dot_general(left, right, (((0,), (0,)), ((), ())), preferred_element_type=f32)


def soft_weights(scores):
    shifted = jnp.exp(scores - jnp.max(scores, axis=-1, keepdims=True))
    return shifted * (1.0 / jnp.sum(shifted, axis=-1, keepdims=True))


def attend_kernel(blocks, bias_ref, mask_ref, q_ref, k_ref, v_ref, o_ref):
    items = [(start, size, masked, head) for start, size, masked in blocks for head in (0, 1)]
    scores = []
    for start, size, masked, head in items:
        rows = pl.ds(start, size)
        part = nt(q_ref[rows, :] * mask_ref[head, :size, :], k_ref[rows, :])
        scores.append(part + bias_ref[...] if masked else part)
    weights = [soft_weights(part).astype(bf16) for part in scores]
    parts = [
        nn(part, v_ref[pl.ds(start, size), :] * mask_ref[2 + head, :size, :])
        for part, (start, size, _, head) in zip(weights, items)
    ]
    for at, (start, size, _) in enumerate(blocks):
        o_ref[pl.ds(start, size), :] = (parts[2 * at] + parts[2 * at + 1]).astype(bf16)


def attend_back_kernel(blocks, slabs, bias_ref, mask_ref, q_ref, k_ref, v_ref, d_ref, o_ref):
    at = pl.program_id(0)
    items = [(start, size, masked, head) for start, size, masked in blocks for head in (0, 1)]
    scores, d_weights = [], []
    for start, size, masked, head in items:
        rows = pl.ds(start, size)
        part = nt(q_ref[rows, :] * mask_ref[head, :size, :], k_ref[rows, :])
        scores.append(part + bias_ref[...] if masked else part)
        d_weights.append(nt(d_ref[rows, :] * mask_ref[2 + head, :size, :], v_ref[rows, :]))
    weights = [soft_weights(part) for part in scores]
    d_scores = [
        (part * (grad - jnp.sum(part * grad, axis=-1, keepdims=True))).astype(bf16)
        for part, grad in zip(weights, d_weights)
    ]
    weights = [part.astype(bf16) for part in weights]
    for index, (start, size, _) in enumerate(blocks):
        rows = pl.ds(start, size)
        dq, dk, dv = 0.0, 0.0, 0.0
        for head in (0, 1):
            scaled, whole = mask_ref[head, :size, :], mask_ref[2 + head, :size, :]
            d_score, weight = d_scores[2 * index + head], weights[2 * index + head]
            dq += nn(d_score, k_ref[rows, :] * scaled)
            dk += tn(d_score, q_ref[rows, :] * scaled)
            dv += tn(weight, d_ref[rows, :] * whole)
        o_ref[rows, pl.ds(at * SLAB, SLAB)] = dq.astype(bf16)
        o_ref[rows, pl.ds((slabs + at) * SLAB, SLAB)] = dk.astype(bf16)
        o_ref[rows, pl.ds((2 * slabs + at) * SLAB, SLAB)] = dv.astype(bf16)


def head_masks(rows):
    low = lax.broadcasted_iota(jnp.int32, (rows, SLAB), 1) < HDIM
    masks = jnp.stack([low, ~low]).astype(bf16)
    return jnp.concatenate([masks * (HDIM**-0.5), masks])


def slab_spec(count, shift):
    return pl.BlockSpec((count, SLAB), lambda i: (0, i + shift))


def attend(packed, bias, masks, blocks):
    count, width = packed.shape
    slabs = width // 3 // SLAB
    flops = sum(4 * size * size * SLAB for _, size, _ in blocks) * 2 * slabs
    return pl.pallas_call(
        functools.partial(attend_kernel, blocks),
        out_shape=jax.ShapeDtypeStruct((count, width // 3), bf16),
        grid=(slabs,),
        in_specs=[
            pl.BlockSpec(bias.shape, lambda i: (0, 0)),
            pl.BlockSpec(masks.shape, lambda i: (0, 0, 0)),
            slab_spec(count, 0),
            slab_spec(count, slabs),
            slab_spec(count, 2 * slabs),
        ],
        out_specs=slab_spec(count, 0),
        cost_estimate=pl.CostEstimate(
            flops=flops, bytes_accessed=count * width * 3, transcendentals=flops // 512
        ),
        compiler_params=pltpu.CompilerParams(vmem_limit_bytes=32 * 2**20),
    )(bias, masks, packed, packed, packed)


def attend_back(packed, upstream, bias, masks, blocks):
    count, width = packed.shape
    slabs = width // 3 // SLAB
    flops = sum(10 * size * size * SLAB for _, size, _ in blocks) * 2 * slabs
    return pl.pallas_call(
        functools.partial(attend_back_kernel, blocks, slabs),
        out_shape=jax.ShapeDtypeStruct((count, width), bf16),
        grid=(slabs,),
        in_specs=[
            pl.BlockSpec(bias.shape, lambda i: (0, 0)),
            pl.BlockSpec(masks.shape, lambda i: (0, 0, 0)),
            slab_spec(count, 0),
            slab_spec(count, slabs),
            slab_spec(count, 2 * slabs),
            slab_spec(count, 0),
        ],
        out_specs=pl.BlockSpec((count, width), lambda i: (0, 0)),
        cost_estimate=pl.CostEstimate(
            flops=flops, bytes_accessed=count * width * 5, transcendentals=flops // 1280
        ),
        compiler_params=pltpu.CompilerParams(vmem_limit_bytes=32 * 2**20),
    )(bias, masks, packed, packed, packed, upstream)


def place_kernel(order, count, me_ref, *refs):
    pieces, out_ref = refs[:count], refs[count]
    for piece, row, kz, ks in order:
        at = jnp.bitwise_xor(me_ref[0], kz), jnp.bitwise_xor(me_ref[1], ks)
        out_ref[at] = pieces[piece][row]


def hold(operand, after):
    return lax.optimization_barrier((operand, after))[0]


def spread_z(shard, dp):
    return jnp.stack([shard] + [swap(shard, "dp", dp, k) for k in range(1, dp)])


def spread_near(block, seq):
    if seq == 4:
        return [swap(block, "seq", seq, 1), swap(block, "seq", seq, 2)]
    return [swap(block, "seq", seq, step) for step in range(1, seq)]


def spread_far(near, seq):
    if seq != 4:
        return []
    from_x, from_y = near
    half = from_x.shape[0] // 2
    return [swap(from_y[:half], "seq", seq, 1), swap(from_x[half:], "seq", seq, 2)]


def place(block, near, far, seq, me):
    dp, rows, width = block.shape
    half = dp // 2
    pieces = [block, *near, *far]
    order = [(index, k, k, index) for index in range(1 + len(near)) for k in range(dp)]
    if far:
        order += [(3, k, k, 3) for k in range(half)]
        order += [(4, k - half, k, 3) for k in range(half, dp)]
    whole = pl.pallas_call(
        functools.partial(place_kernel, order, len(pieces)),
        out_shape=jax.ShapeDtypeStruct((dp, seq, rows, width), block.dtype),
        grid=(width // COLUMNS,),
        in_specs=[pl.BlockSpec(memory_space=pltpu.SMEM)]
        + [
            pl.BlockSpec((piece.shape[0], rows, COLUMNS), lambda i: (0, 0, i)) for piece in pieces
        ],
        out_specs=pl.BlockSpec((dp, seq, rows, COLUMNS), lambda i: (0, 0, 0, i)),
        cost_estimate=pl.CostEstimate(
            flops=0, bytes_accessed=4 * dp * seq * rows * width, transcendentals=0
        ),
        compiler_params=pltpu.CompilerParams(vmem_limit_bytes=32 * 2**20),
    )(me, *pieces)
    whole = whole.reshape(dp * seq * rows, width)
    return [whole, swap(whole, "tensor", 2, 1)]


def grad_block(index, split, left_refs, right_refs):
    if len(left_refs) == 1:
        return tn(left_refs[0][...], right_refs[0][...])
    return lax.cond(
        index < split,
        lambda: tn(left_refs[0][...], right_refs[0][...]),
        lambda: tn(left_refs[1][...], right_refs[1][...]),
    )


def grad_kernel(pairs, split, *refs):
    left, right, out_ref = refs[:pairs], refs[pairs : 2 * pairs], refs[-1]
    out_ref[...] = grad_block(pl.program_id(0), split, left, right).astype(bf16)


def grad_parts_kernel(pairs, split, dp, seq, me_ref, *refs):
    left, right, other_ref = refs[:pairs], refs[pairs : 2 * pairs], refs[2 * pairs]
    outs = refs[2 * pairs + 1 :]
    total = grad_block(pl.program_id(0), split, left, right) + other_ref[...].astype(f32)
    total = total.astype(bf16)
    rows = total.shape[0] // (dp * seq)
    for owner in range(seq):
        step = jnp.bitwise_xor(me_ref[1], owner)
        parts = [total[(z * seq + owner) * rows :][:rows] for z in range(dp)]
        for k in range(seq):

            @pl.when(step == k)
            def _():
                for z in range(dp):
                    if seq == 4 and k == 3:
                        outs[3 + z // (dp // 2)][z % (dp // 2)] = parts[z]
                    else:
                        outs[k][z] = parts[z]


COLUMNS = 512


def grad_specs(left, right):
    rows = left[0].shape[0]
    split = right[0].shape[1] // COLUMNS
    specs = [pl.BlockSpec(member.shape, lambda i: (0, 0)) for member in left]
    specs.append(pl.BlockSpec((rows, COLUMNS), lambda i: (0, jnp.minimum(i, split - 1))))
    if len(right) > 1:
        specs.append(pl.BlockSpec((rows, COLUMNS), lambda i: (0, jnp.maximum(i - split, 0))))
    width = sum(member.shape[1] for member in right)
    cost = pl.CostEstimate(
        flops=2 * rows * left[0].shape[1] * width,
        bytes_accessed=2 * width * left[0].shape[1] * 2,
        transcendentals=0,
    )
    return split, specs, width, cost


def grad_other(left, right):
    split, specs, width, cost = grad_specs(left, right)
    features = left[0].shape[1]
    return pl.pallas_call(
        functools.partial(grad_kernel, len(left), split),
        out_shape=jax.ShapeDtypeStruct((features, width), bf16),
        grid=(width // COLUMNS,),
        in_specs=specs,
        out_specs=pl.BlockSpec((features, COLUMNS), lambda i: (0, i)),
        cost_estimate=cost,
        compiler_params=pltpu.CompilerParams(vmem_limit_bytes=32 * 2**20),
    )(*left, *right)


def grad_parts(left, right, other, sizes, me):
    dp, seq = sizes
    split, specs, width, cost = grad_specs(left, right)
    features = left[0].shape[1]
    rows = features // (dp * seq)
    depths = [dp] * seq if seq != 4 else [dp, dp, dp, dp // 2, dp - dp // 2]
    return pl.pallas_call(
        functools.partial(grad_parts_kernel, len(left), split, dp, seq),
        out_shape=[jax.ShapeDtypeStruct((depth, rows, width), bf16) for depth in depths],
        grid=(width // COLUMNS,),
        in_specs=[
            pl.BlockSpec(memory_space=pltpu.SMEM),
            *specs,
            pl.BlockSpec((features, COLUMNS), lambda i: (0, i)),
        ],
        out_specs=[pl.BlockSpec((depth, rows, COLUMNS), lambda i: (0, 0, i)) for depth in depths],
        cost_estimate=cost,
        compiler_params=pltpu.CompilerParams(vmem_limit_bytes=32 * 2**20),
    )(me, *left, *right, other)


def reduce_far(parts, seq):
    if seq != 4:
        return parts[0], parts[1:]
    own, to_x, to_y, low, high = parts
    half = low.shape[0]
    from_x, from_y = swap(low, "seq", seq, 1), swap(high, "seq", seq, 2)
    to_x = jnp.concatenate([to_x[:half], to_x[half:] + from_y])
    to_y = jnp.concatenate([to_y[:half] + from_x, to_y[half:]])
    return own, [to_x, to_y]


def sum_kernel(count, dp, me_ref, *refs):
    parts, outs = refs[:count], refs[count:]
    for z in range(dp):
        total = sum(part[z].astype(f32) for part in parts).astype(bf16)
        for k in range(dp):

            @pl.when(jnp.bitwise_xor(me_ref[0], z) == k)
            def _():
                outs[k][...] = total


def reduce_near(state, sizes, me):
    dp, seq = sizes
    own, sends = state
    parts = [own] + [swap(part, "seq", seq, 1 + step) for step, part in enumerate(sends)]
    rows, width = own.shape[1:]
    spec = pl.BlockSpec((dp, rows, COLUMNS), lambda i: (0, 0, i))
    return pl.pallas_call(
        functools.partial(sum_kernel, len(parts), dp),
        out_shape=[jax.ShapeDtypeStruct((rows, width), bf16)] * dp,
        grid=(width // COLUMNS,),
        in_specs=[pl.BlockSpec(memory_space=pltpu.SMEM)] + [spec] * len(parts),
        out_specs=[pl.BlockSpec((rows, COLUMNS), lambda i: (0, i))] * dp,
        cost_estimate=pl.CostEstimate(
            flops=0, bytes_accessed=2 * (len(parts) + 1) * dp * rows * width, transcendentals=0
        ),
        compiler_params=pltpu.CompilerParams(vmem_limit_bytes=32 * 2**20),
    )(me, *parts)


def reduce_z(parts, dp):
    return sum(
        [parts[0].astype(f32)] + [swap(parts[k], "dp", dp, k).astype(f32) for k in range(1, dp)]
    )


def xor_onehot(count, rank):
    index = lax.broadcasted_iota(jnp.int32, (count, count), 0)
    other = lax.broadcasted_iota(jnp.int32, (count, count), 1)
    return (jnp.bitwise_xor(index, rank) == other).astype(f32)


def gather_vectors(shard, sizes, rank):
    dp, seq = sizes
    rows, width = shard.shape
    found = jnp.stack([shard, swap(shard, "tensor", 2, 1)])
    found = jnp.stack([found] + [swap(found, "seq", seq, k) for k in range(1, seq)])
    found = jnp.stack([found] + [swap(found, "dp", dp, k) for k in range(1, dp)])
    count = dp * seq * 2
    found = found.reshape(count, rows * width).astype(f32)
    placed = jnp.dot(xor_onehot(count, rank), found, precision=highest)
    return placed.reshape(count, rows, width).transpose(1, 0, 2).reshape(rows, count * width)


def reduce_vectors(whole, sizes, rank):
    dp, seq = sizes
    rows, features = whole.shape
    count = dp * seq * 2
    width = features // count
    parts = whole.reshape(rows, count, width).transpose(1, 0, 2).reshape(count, rows * width)
    parts = jnp.dot(xor_onehot(count, rank), parts, precision=highest)
    parts = parts.reshape(dp, seq, 2, rows * width)
    total = parts[0]
    for step in range(1, dp):
        total = total + swap(parts[step], "dp", dp, step)
    parts, total = total, total[0]
    for step in range(1, seq):
        total = total + swap(parts[step], "seq", seq, step)
    total = total[0] + swap(total[1], "tensor", 2, 1)
    return total.reshape(rows, width)


def turn(operand, axis, size, rank):
    bit = 1
    shape = operand.shape
    while bit < size:
        split = operand.reshape(shape[:axis] + (size // (2 * bit), 2, bit) + shape[axis + 1 :])
        low, high = [lax.index_in_dim(split, at, axis + 1, keepdims=False) for at in (0, 1)]
        moved = jnp.bitwise_and(rank, bit) != 0
        both = [jnp.where(moved, high, low), jnp.where(moved, low, high)]
        operand = jnp.stack(both, axis=axis + 1).reshape(shape)
        bit *= 2
    return operand


def enter(first, second, seq, me):
    s, t = me[1], me[2]
    shapes = [member.shape for member in (first, second)]

    def pick(which):
        return jnp.concatenate(
            [
                lax.dynamic_index_in_dim(member, which, 0, keepdims=False).reshape(-1, shape[3])
                for member, shape in zip((first, second), shapes)
            ]
        )

    own, received = pick(t), swap(pick(1 - t), "tensor", 2, 1)
    rows, start = [], 0
    for shape in shapes:
        frames, places, features = shape[1:]
        stop = start + frames * places
        halves = [
            member[start:stop].reshape(frames, seq, places // seq, features)
            for member in (own, received)
        ]
        rows.append(turn(jnp.concatenate(halves, axis=2), 1, seq, s).reshape(-1, features))
        start = stop
    return jnp.concatenate(rows)


def leave(tokens, shapes, seq, me):
    s, t = me[1], me[2]
    features = tokens.shape[1]
    own, other, start = [], [], 0
    for shape in shapes:
        frames, places = shape[1:3]
        stop = start + 2 * frames * places
        member = turn(
            tokens[start:stop].reshape(frames, seq, 2, places // seq, features), 1, seq, s
        )
        own.append(member[:, :, 0].reshape(-1, features))
        other.append(member[:, :, 1].reshape(-1, features))
        start = stop
    own, received = jnp.concatenate(own), swap(jnp.concatenate(other), "tensor", 2, 1)
    results, start = [], 0
    for shape in shapes:
        frames, places = shape[1:3]
        stop = start + frames * places
        mine, theirs = own[start:stop], received[start:stop]
        both = jnp.stack([jnp.where(t == 0, mine, theirs), jnp.where(t == 0, theirs, mine)])
        results.append(both.reshape(shape))
        start = stop
    return results


def to_places(tokens, counts, seq):
    features = tokens.shape[1]
    members, start = [], 0
    for frames, places in counts:
        stop = start + frames * places
        members.append(tokens[start:stop].reshape(frames, seq, places // seq, features))
        start = stop
    pieces = [
        jnp.concatenate([member[:, step].reshape(-1, features) for member in members])
        for step in range(seq)
    ]
    pieces = jnp.stack(
        [pieces[0]] + [swap(pieces[step], "seq", seq, step) for step in range(1, seq)]
    )
    rows, start = [], 0
    for frames, places in counts:
        local = places // seq
        group = BLOCK // (frames * seq)
        stop = start + frames * local
        member = pieces[:, start:stop].reshape(seq, frames, local // group, group, features)
        rows.append(member.transpose(2, 0, 1, 3, 4).reshape(-1, features))
        start = stop
    return jnp.concatenate(rows)


def to_frames(tokens, counts, seq):
    features = tokens.shape[1]
    members, start = [], 0
    for frames, places in counts:
        local = places // seq
        group = BLOCK // (frames * seq)
        stop = start + seq * frames * local
        member = tokens[start:stop].reshape(local // group, seq, frames, group, features)
        members.append(member.transpose(1, 2, 0, 3, 4).reshape(seq, -1, features))
        start = stop
    pieces = jnp.concatenate(members, axis=1)
    pieces = jnp.stack(
        [pieces[0]] + [swap(pieces[step], "seq", seq, step) for step in range(1, seq)]
    )
    rows, start = [], 0
    for frames, places in counts:
        local = places // seq
        stop = start + frames * local
        member = pieces[:, start:stop].reshape(seq, frames, local, features)
        rows.append(member.transpose(1, 0, 2, 3).reshape(-1, features))
        start = stop
    return jnp.concatenate(rows)


def allowed_bias(allowed):
    return jnp.where(allowed, 0.0, masked_score).astype(f32)


ROOT = 0.7978845608028654
CUBE = 0.044715


def ffn_kernel(n_ref, c_ref, up_ref, down_ref, z_ref, du_ref, mixed_ref, dn_ref):
    @pl.when(pl.program_id(0) == 0)
    def _():
        mixed_ref[...] = jnp.zeros_like(mixed_ref)
        dn_ref[...] = jnp.zeros_like(dn_ref)

    u = nn(n_ref[...], up_ref[...])
    da = nn(c_ref[...], down_ref[...])
    square = u * u
    bent = jnp.tanh(u * (ROOT + ROOT * CUBE * square))
    half = 0.5 + 0.5 * bent
    z = (u * half).astype(bf16)
    slope = half + (0.5 * u) * (1.0 - bent * bent) * (ROOT + 3.0 * ROOT * CUBE * square)
    du = (da * slope).astype(bf16)
    z_ref[...] = z
    du_ref[...] = du
    mixed_ref[...] += nt(z, down_ref[...])
    dn_ref[...] += nt(du, up_ref[...])


def ffn(normed, cotangent, up, down):
    count, features = normed.shape
    hidden = up.shape[1]
    rows = pl.BlockSpec((count, features), lambda i: (0, 0))
    weight = pl.BlockSpec((features, COLUMNS), lambda i: (0, i))
    units = pl.BlockSpec((count, COLUMNS), lambda i: (0, i))
    return pl.pallas_call(
        ffn_kernel,
        out_shape=[jax.ShapeDtypeStruct((count, hidden), bf16)] * 2
        + [jax.ShapeDtypeStruct((count, features), f32)] * 2,
        grid=(hidden // COLUMNS,),
        in_specs=[rows, rows, weight, weight],
        out_specs=[units, units, rows, rows],
        cost_estimate=pl.CostEstimate(
            flops=8 * count * features * hidden,
            bytes_accessed=4 * features * hidden,
            transcendentals=count * hidden,
        ),
        compiler_params=pltpu.CompilerParams(vmem_limit_bytes=48 * 2**20),
    )(normed, cotangent, up, down)


def project(rows, half, stop):
    return jnp.dot(rows, half[:, :stop], preferred_element_type=f32).astype(bf16)


def project_out(mixed, halves, start):
    return sum(nt(member, half[:, start:]) for member, half in zip(mixed, halves))


def pull_out(gradient, half, start):
    return jnp.dot(gradient, half[:, start:], preferred_element_type=f32).astype(bf16)


def pull_in(packed, halves, stop):
    return sum(nt(member, half[:, :stop]) for member, half in zip(packed, halves))


def local(
    sizes,
    clips_a,
    actions_a,
    clips_b,
    actions_b,
    space_in,
    space_out,
    time_in,
    time_out,
    ffn_up,
    ffn_down,
    norm_gain,
    norm_shift,
    action_table,
    cot_a,
    cot_b,
):
    dp, seq = sizes
    me = [lax.axis_index(name) for name in ("dp", "seq", "tensor")]
    rank = (me[0] * seq + me[1]) * 2 + me[2]
    me_array = jnp.stack(me).astype(jnp.int32)
    rows_in, wide = space_in.shape[1], 3 * space_in.shape[2]

    def pack(inward, outward):
        return jnp.concatenate([inward.transpose(1, 0, 2).reshape(rows_in, wide), outward], axis=1)

    shapes = [clips_a.shape, clips_b.shape]
    frames = clips_a.shape[1]
    counts = [(shape[1], 2 * shape[2]) for shape in shapes]

    clips = enter(clips_a, clips_b, seq, me)
    vectors = gather_vectors(
        jnp.concatenate([norm_gain, norm_shift, action_table]), sizes, rank
    )
    space_block = spread_z(pack(space_in, space_out), dp)
    cot = to_places(enter(cot_a, cot_b, seq, me), counts, seq)
    time_block = spread_z(hold(pack(time_in, time_out), space_block), dp)
    space_near = spread_near(space_block, seq)
    time_block = hold(time_block, (space_near, cot))
    up_block = spread_z(hold(ffn_up, time_block), dp)
    space = place(space_block, space_near, spread_far(space_near, seq), seq, me_array)
    time_near = spread_near(time_block, seq)
    up_block = hold(up_block, time_near)
    down_block = spread_z(hold(ffn_down, up_block), dp)
    time = place(time_block, time_near, spread_far(time_near, seq), seq, me_array)
    up_near = spread_near(up_block, seq)
    down_block = hold(down_block, up_near)
    up = place(up_block, up_near, spread_far(up_near, seq), seq, me_array)
    down_near = spread_near(down_block, seq)
    down = place(down_block, down_near, spread_far(down_near, seq), seq, me_array)

    gains, shifts, table = vectors[:3], vectors[3:6], vectors[6:]
    acts = jnp.concatenate(
        [
            lax.dynamic_index_in_dim(member, me[2], 0, keepdims=False)
            for member in (actions_a, actions_b)
        ]
    )
    onehot = (
        acts[:, None] == lax.broadcasted_iota(jnp.int32, (1, table.shape[0]), 1)
    ).astype(f32)
    rows_of = jnp.dot(onehot, table, precision=highest)
    spread = jnp.concatenate(
        [
            jnp.broadcast_to(
                rows_of[index * frames : (index + 1) * frames, None, :],
                (frames, places, table.shape[1]),
            ).reshape(-1, table.shape[1])
            for index, (_, places) in enumerate(counts)
        ]
    )
    entered = clips.astype(f32) + spread

    places_a, places_b = counts[0][1], counts[1][1]
    space_blocks = [(frame * places_a, places_a, False) for frame in range(frames)]
    space_blocks.append((frames * places_a, frames * places_b, True))
    index = lax.broadcasted_iota(jnp.int32, (frames * places_b, 1), 0) // places_b
    space_bias = allowed_bias(index == index.reshape(1, -1))
    total_tokens = clips.shape[0]
    time_blocks = [(start, BLOCK, True) for start in range(0, total_tokens, BLOCK)]
    group = BLOCK // (frames * seq)
    token = lax.broadcasted_iota(jnp.int32, (BLOCK, 1), 0)
    spot = token % group
    frame_id = (
        jnp.bitwise_xor(token // (frames * group), me[1]) * frames + (token // group) % frames
    )
    time_bias = allowed_bias(
        (spot == spot.reshape(1, -1)) & (frame_id.reshape(1, -1) <= frame_id)
    )

    masks = head_masks(max(BLOCK, places_a))

    normed_one = layer_norm(entered, gains[0], shifts[0])
    packed_one = [project(normed_one, half, wide) for half in space]
    mixed_one = [attend(member, space_bias, masks, space_blocks) for member in packed_one]
    middle = entered + project_out(mixed_one, space, wide)
    middle = to_places(middle.astype(bf16), counts, seq).astype(f32)
    normed_two = layer_norm(middle, gains[1], shifts[1])
    packed_two = [project(normed_two, half, wide) for half in time]
    mixed_two = [attend(member, time_bias, masks, time_blocks) for member in packed_two]
    before = middle + project_out(mixed_two, time, wide)
    normed_three = layer_norm(before, gains[2], shifts[2])
    act_own, du_own, mixed_own, dn_own = ffn(normed_three, cot, up[0], down[0])
    act_other, du_other, mixed_other, dn_other = ffn(normed_three, cot, up[1], down[1])
    mixed = to_frames((before + mixed_own + mixed_other).astype(bf16), counts, seq)

    down_other = swap(grad_other([cot], [act_other]), "tensor", 2, 1)
    up_other = swap(grad_other([normed_three], [du_other]), "tensor", 2, 1)
    down_parts = grad_parts([cot], [act_own], down_other, sizes, me_array)
    down_parts, mixed = lax.optimization_barrier((down_parts, mixed))
    mixed = leave(mixed, shapes, seq, me)
    up_parts = grad_parts([normed_three], [du_own], up_other, sizes, me_array)
    dn_own, up_parts = lax.optimization_barrier((dn_own, up_parts))

    d_input, gain_three, shift_three = norm_back(before, gains[2], dn_own + dn_other)
    gradient = cot.astype(f32) + d_input
    rounded = gradient.astype(bf16)
    down_state = reduce_far(down_parts, seq)
    rounded, down_state = lax.optimization_barrier((rounded, down_state))
    up_state = reduce_far(up_parts, seq)
    upstream = [pull_out(rounded, half, wide) for half in time]
    d_own = attend_back(packed_two[0], upstream[0], time_bias, masks, time_blocks)
    upstream[1], up_state = lax.optimization_barrier((upstream[1], up_state))
    d_other = attend_back(packed_two[1], upstream[1], time_bias, masks, time_blocks)
    d_packed = [d_own, d_other]
    down_rows = reduce_near(down_state, sizes, me_array)
    d_packed, down_rows, up_state = lax.optimization_barrier((d_packed, down_rows, up_state))
    d_input, gain_two, shift_two = norm_back(middle, gains[1], pull_in(d_packed, time, wide))
    rounded_two = to_frames((gradient + d_input).astype(bf16), counts, seq)
    time_other = swap(
        grad_other([normed_two, rounded], [d_packed[1], mixed_two[1]]), "tensor", 2, 1
    )
    time_parts = grad_parts(
        [normed_two, rounded], [d_packed[0], mixed_two[0]], time_other, sizes, me_array
    )
    up_rows = reduce_near(up_state, sizes, me_array)
    rounded, time_parts, up_rows = lax.optimization_barrier((rounded_two, time_parts, up_rows))
    grad_down = reduce_z(down_rows, dp)
    time_state = reduce_far(time_parts, seq)
    upstream = [pull_out(rounded, half, wide) for half in space]
    upstream, time_state = lax.optimization_barrier((upstream, time_state))
    d_own = attend_back(packed_one[0], upstream[0], space_bias, masks, space_blocks)
    d_other = attend_back(packed_one[1], upstream[1], space_bias, masks, space_blocks)
    d_packed = [d_own, d_other]
    space_other = swap(
        grad_other([normed_one, rounded], [d_packed[1], mixed_one[1]]), "tensor", 2, 1
    )
    time_rows = reduce_near(time_state, sizes, me_array)
    grad_up = reduce_z(up_rows, dp)
    space_parts = grad_parts(
        [normed_one, rounded], [d_packed[0], mixed_one[0]], space_other, sizes, me_array
    )
    space_parts, time_rows, grad_down, grad_up = lax.optimization_barrier(
        (space_parts, time_rows, grad_down, grad_up)
    )
    space_state = reduce_far(space_parts, seq)
    grad_time = reduce_z(time_rows, dp)
    d_input, gain_one, shift_one = norm_back(entered, gains[0], pull_in(d_packed, space, wide))
    gradient = rounded.astype(f32) + d_input
    sums, start = [], 0
    for frame_count, places in counts:
        stop = start + frame_count * places
        sums.append(jnp.sum(gradient[start:stop].reshape(frame_count, places, -1), axis=1))
        start = stop
    grad_table = jnp.dot(onehot.T, jnp.concatenate(sums), precision=highest)
    vector_grads = reduce_vectors(
        jnp.concatenate(
            [
                jnp.stack([gain_one, gain_two, gain_three, shift_one, shift_two, shift_three]),
                grad_table,
            ]
        ),
        sizes,
        rank,
    )
    grads = leave(gradient.astype(bf16), shapes, seq, me)
    grad_space = reduce_z(reduce_near(space_state, sizes, me_array), dp)

    def unpack(member):
        inward = member[:, :wide].reshape(rows_in, 3, -1).transpose(1, 0, 2)
        return inward, member[:, wide:]

    return (
        *mixed,
        *grads,
        *unpack(grad_space),
        *unpack(grad_time),
        grad_up,
        grad_down,
        vector_grads[:3],
        vector_grads[3:6],
        vector_grads[6:],
    )


def solution(mesh):
    sizes = (mesh.shape["dp"], mesh.shape["seq"])
    in_specs = (
        P("dp", "seq", "tensor", None),
        P("dp", "seq"),
        P("dp", "seq", "tensor", None),
        P("dp", "seq"),
        P(None, ("dp", "seq"), "tensor"),
        P(("dp", "seq"), "tensor"),
        P(None, ("dp", "seq"), "tensor"),
        P(("dp", "seq"), "tensor"),
        P(("dp", "seq"), "tensor"),
        P(("dp", "seq"), "tensor"),
        P(None, ("dp", "seq", "tensor")),
        P(None, ("dp", "seq", "tensor")),
        P(None, ("dp", "seq", "tensor")),
        P("dp", "seq", "tensor", None),
        P("dp", "seq", "tensor", None),
    )
    out_specs = (
        P("dp", "seq", "tensor", None),
        P("dp", "seq", "tensor", None),
        P("dp", "seq", "tensor", None),
        P("dp", "seq", "tensor", None),
        P(None, ("dp", "seq"), "tensor"),
        P(("dp", "seq"), "tensor"),
        P(None, ("dp", "seq"), "tensor"),
        P(("dp", "seq"), "tensor"),
        P(("dp", "seq"), "tensor"),
        P(("dp", "seq"), "tensor"),
        P(None, ("dp", "seq", "tensor")),
        P(None, ("dp", "seq", "tensor")),
        P(None, ("dp", "seq", "tensor")),
    )
    return jax.shard_map(
        functools.partial(local, sizes),
        mesh=mesh,
        in_specs=in_specs,
        out_specs=out_specs,
        check_vma=False,
    )
```

```python
import functools

import jax
import jax.numpy as jnp
from jax import lax
from jax.experimental import pallas as pl
from jax.experimental.pallas import tpu as pltpu
from jax.sharding import PartitionSpec as P

HDIM = 64
BLOCK = 128

epsilon = 1e-05
masked_score = -1e30
highest = lax.Precision.HIGHEST
bf16 = jnp.bfloat16
f32 = jnp.float32


def swap(operand, axis, size, step):
    return lax.ppermute(operand, axis, [(i, i ^ step) for i in range(size)])


def norm_stats(operand):
    centred = operand - jnp.mean(operand, axis=-1, keepdims=True)
    inverse = lax.rsqrt(jnp.mean(centred * centred, axis=-1, keepdims=True) + epsilon)
    return centred * inverse, inverse


def layer_norm(operand, gain_row, shift_row):
    standard, _ = norm_stats(operand)
    return (standard * gain_row + shift_row).astype(bf16)


def norm_back(operand, gain_row, upstream):
    standard, inverse = norm_stats(operand)
    scaled = upstream * gain_row
    inner = (
        scaled
        - jnp.mean(scaled, axis=-1, keepdims=True)
        - standard * jnp.mean(scaled * standard, axis=-1, keepdims=True)
    )
    return inverse * inner, jnp.sum(upstream * standard, axis=0), jnp.sum(upstream, axis=0)


SLAB = 2 * HDIM


def nt(left, right):
    return lax.dot_general(left, right, (((1,), (1,)), ((), ())), preferred_element_type=f32)


def nn(left, right):
    return lax.dot_general(left, right, (((1,), (0,)), ((), ())), preferred_element_type=f32)


def tn(left, right):
    return lax.dot_general(left, right, (((0,), (0,)), ((), ())), preferred_element_type=f32)


def soft_weights(scores):
    shifted = jnp.exp(scores - jnp.max(scores, axis=-1, keepdims=True))
    return shifted * (1.0 / jnp.sum(shifted, axis=-1, keepdims=True))


def attend_kernel(blocks, bias_ref, mask_ref, p_ref, o_ref):
    items = [(start, size, masked, head) for start, size, masked in blocks for head in (0, 1)]
    scores = []
    for start, size, masked, head in items:
        rows = pl.ds(start, size)
        part = nt(p_ref[rows, :SLAB] * mask_ref[head, :size, :], p_ref[rows, SLAB : 2 * SLAB])
        scores.append(part + bias_ref[...] if masked else part)
    weights = [soft_weights(part).astype(bf16) for part in scores]
    parts = [
        nn(part, p_ref[pl.ds(start, size), 2 * SLAB :] * mask_ref[2 + head, :size, :])
        for part, (start, size, _, head) in zip(weights, items)
    ]
    for at, (start, size, _) in enumerate(blocks):
        o_ref[pl.ds(start, size), :] = (parts[2 * at] + parts[2 * at + 1]).astype(bf16)


def attend_back_kernel(blocks, bias_ref, mask_ref, p_ref, d_ref, o_ref):
    items = [(start, size, masked, head) for start, size, masked in blocks for head in (0, 1)]
    scores, d_weights = [], []
    for start, size, masked, head in items:
        rows = pl.ds(start, size)
        part = nt(p_ref[rows, :SLAB] * mask_ref[head, :size, :], p_ref[rows, SLAB : 2 * SLAB])
        scores.append(part + bias_ref[...] if masked else part)
        d_weights.append(nt(d_ref[rows, :] * mask_ref[2 + head, :size, :], p_ref[rows, 2 * SLAB :]))
    weights = [soft_weights(part) for part in scores]
    d_scores = [
        (part * (grad - jnp.sum(part * grad, axis=-1, keepdims=True))).astype(bf16)
        for part, grad in zip(weights, d_weights)
    ]
    weights = [part.astype(bf16) for part in weights]
    for index, (start, size, _) in enumerate(blocks):
        rows = pl.ds(start, size)
        dq, dk, dv = 0.0, 0.0, 0.0
        for head in (0, 1):
            scaled, whole = mask_ref[head, :size, :], mask_ref[2 + head, :size, :]
            d_score, weight = d_scores[2 * index + head], weights[2 * index + head]
            dq += nn(d_score, p_ref[rows, SLAB : 2 * SLAB] * scaled)
            dk += tn(d_score, p_ref[rows, :SLAB] * scaled)
            dv += tn(weight, d_ref[rows, :] * whole)
        o_ref[rows, :SLAB] = dq.astype(bf16)
        o_ref[rows, SLAB : 2 * SLAB] = dk.astype(bf16)
        o_ref[rows, 2 * SLAB :] = dv.astype(bf16)


def head_masks(rows):
    low = lax.broadcasted_iota(jnp.int32, (rows, SLAB), 1) < HDIM
    masks = jnp.stack([low, ~low]).astype(bf16)
    return jnp.concatenate([masks * (HDIM**-0.5), masks])


def slab_spec(count, width):
    return pl.BlockSpec((count, width), lambda i: (0, i))


def attend_specs(packed, bias, masks, blocks, products):
    count, width = packed.shape
    slabs = width // (3 * SLAB)
    specs = [
        pl.BlockSpec(bias.shape, lambda i: (0, 0)),
        pl.BlockSpec(masks.shape, lambda i: (0, 0, 0)),
        slab_spec(count, 3 * SLAB),
    ]
    scores = 2 * slabs * sum(size * size for _, size, _ in blocks)
    cost = pl.CostEstimate(
        flops=2 * products * scores * SLAB,
        bytes_accessed=count * width * products,
        transcendentals=scores,
    )
    return count, slabs, specs, cost


def attend(packed, bias, masks, blocks):
    count, slabs, specs, cost = attend_specs(packed, bias, masks, blocks, 2)
    return pl.pallas_call(
        functools.partial(attend_kernel, blocks),
        out_shape=jax.ShapeDtypeStruct((count, slabs * SLAB), bf16),
        grid=(slabs,),
        in_specs=specs,
        out_specs=slab_spec(count, SLAB),
        cost_estimate=cost,
        compiler_params=pltpu.CompilerParams(vmem_limit_bytes=32 * 2**20),
    )(bias, masks, packed)


def attend_back(packed, upstream, bias, masks, blocks):
    count, slabs, specs, cost = attend_specs(packed, bias, masks, blocks, 5)
    return pl.pallas_call(
        functools.partial(attend_back_kernel, blocks),
        out_shape=jax.ShapeDtypeStruct(packed.shape, bf16),
        grid=(slabs,),
        in_specs=[*specs, slab_spec(count, SLAB)],
        out_specs=slab_spec(count, 3 * SLAB),
        cost_estimate=cost,
        compiler_params=pltpu.CompilerParams(vmem_limit_bytes=32 * 2**20),
    )(bias, masks, packed, upstream)


def place_kernel(order, count, relative, me_ref, *refs):
    pieces, out_ref = refs[:count], refs[count]
    for piece, row, kz, ks in order:
        at_z = jnp.bitwise_xor(me_ref[0], kz) if relative else kz
        at = at_z, jnp.bitwise_xor(me_ref[1], ks)
        out_ref[at] = pieces[piece][row]


def phase(*state):
    return lax.optimization_barrier(state)


def double_z(state, step, dp):
    return jnp.concatenate([state, swap(state, "dp", dp, step)])


def parts_z(shard, dp):
    return [shard] + [swap(shard, "dp", dp, k) for k in range(1, dp)]


def spread_z(state, step, dp):
    while step < dp:
        state = double_z(state, step, dp)
        step *= 2
    return state


def spread_near(block, seq):
    if seq == 4:
        return [swap(block, "seq", seq, 1), swap(block, "seq", seq, 2)]
    return [swap(block, "seq", seq, step) for step in range(1, seq)]


def spread_far(near, seq):
    if seq != 4:
        return []
    from_x, from_y = near
    half = from_x.shape[0] // 2
    return [swap(from_y[:half], "seq", seq, 1), swap(from_x[half:], "seq", seq, 2)]


def place(block, near, far, seq, me, relative=True):
    dp, rows, width = block.shape
    half = dp // 2
    pieces = [block, *near, *far]
    order = [(index, k, k, index) for index in range(1 + len(near)) for k in range(dp)]
    if far:
        order += [(3, k, k, 3) for k in range(half)]
        order += [(4, k - half, k, 3) for k in range(half, dp)]
    whole = pl.pallas_call(
        functools.partial(place_kernel, order, len(pieces), relative),
        out_shape=jax.ShapeDtypeStruct((dp, seq, rows, width), block.dtype),
        grid=(width // COLUMNS,),
        in_specs=[pl.BlockSpec(memory_space=pltpu.SMEM)]
        + [
            pl.BlockSpec((piece.shape[0], rows, COLUMNS), lambda i: (0, 0, i)) for piece in pieces
        ],
        out_specs=pl.BlockSpec((dp, seq, rows, COLUMNS), lambda i: (0, 0, 0, i)),
        cost_estimate=pl.CostEstimate(
            flops=0, bytes_accessed=4 * dp * seq * rows * width, transcendentals=0
        ),
        compiler_params=pltpu.CompilerParams(vmem_limit_bytes=32 * 2**20),
    )(me, *pieces)
    return whole.reshape(dp * seq * rows, width)


def each_block(pairs, splits, left, right, store):
    at = pl.program_id(0)
    if pairs == 1:
        store(tn(left[0][...], right[0][...]))
        return
    for pair in range(pairs):

        @pl.when((at >= splits[pair]) & (at < splits[pair + 1]))
        def _():
            store(tn(left[pair][...], right[pair][...]))


def grad_kernel(pairs, splits, *refs):
    left, right, out_ref = refs[:pairs], refs[pairs : 2 * pairs], refs[-1]

    def store(total):
        out_ref[...] = total.astype(bf16)

    each_block(pairs, splits, left, right, store)


def grad_parts_kernel(pairs, splits, dp, seq, me_ref, *refs):
    left, right, other_ref = refs[:pairs], refs[pairs : 2 * pairs], refs[2 * pairs]
    outs, held = refs[2 * pairs + 1 : -1], refs[-1]
    rows = other_ref.shape[0] // (dp * seq)

    def store(total):
        total = total + other_ref[...].astype(f32)
        held[...] = total.astype(bf16).reshape(held.shape)

    each_block(pairs, splits, left, right, store)
    for k in range(seq):
        owner = jnp.bitwise_xor(me_ref[1], k)
        for z in range(dp):
            part = held[z * seq + owner]
            if seq == 4 and k == 3:
                outs[3 + z // (dp // 2)][z % (dp // 2)] = part
            else:
                outs[k][z] = part


COLUMNS = 512


def grad_specs(left, right):
    rows, features = left[0].shape
    splits = [0]
    for member in right:
        splits.append(splits[-1] + member.shape[1] // COLUMNS)
    specs = [pl.BlockSpec(member.shape, lambda i: (0, 0)) for member in left]

    def columns(first, last):
        return lambda i: (0, jnp.clip(i - first, 0, last - first - 1))

    for first, last in zip(splits, splits[1:]):
        specs.append(pl.BlockSpec((rows, COLUMNS), columns(first, last)))
    width = splits[-1] * COLUMNS
    cost = pl.CostEstimate(
        flops=2 * rows * features * width,
        bytes_accessed=4 * width * features,
        transcendentals=0,
    )
    return splits, specs, width, cost


def grad_other(left, right):
    splits, specs, width, cost = grad_specs(left, right)
    features = left[0].shape[1]
    return pl.pallas_call(
        functools.partial(grad_kernel, len(left), splits),
        out_shape=jax.ShapeDtypeStruct((features, width), bf16),
        grid=(width // COLUMNS,),
        in_specs=specs,
        out_specs=pl.BlockSpec((features, COLUMNS), lambda i: (0, i)),
        cost_estimate=cost,
        compiler_params=pltpu.CompilerParams(vmem_limit_bytes=32 * 2**20),
    )(*left, *right)


def grad_parts(left, right, other, sizes, me):
    dp, seq = sizes
    splits, specs, width, cost = grad_specs(left, right)
    features = left[0].shape[1]
    rows = features // (dp * seq)
    depths = [dp] * seq if seq != 4 else [dp, dp, dp, dp // 2, dp - dp // 2]
    return pl.pallas_call(
        functools.partial(grad_parts_kernel, len(left), splits, dp, seq),
        out_shape=[jax.ShapeDtypeStruct((depth, rows, width), bf16) for depth in depths],
        grid=(width // COLUMNS,),
        in_specs=[
            pl.BlockSpec(memory_space=pltpu.SMEM),
            *specs,
            pl.BlockSpec((features, COLUMNS), lambda i: (0, i)),
        ],
        out_specs=[pl.BlockSpec((depth, rows, COLUMNS), lambda i: (0, 0, i)) for depth in depths],
        scratch_shapes=[pltpu.VMEM((dp * seq, rows, COLUMNS), bf16)],
        cost_estimate=cost,
        compiler_params=pltpu.CompilerParams(vmem_limit_bytes=40 * 2**20),
    )(me, *left, *right, other)


def reduce_far(parts, seq):
    if seq != 4:
        return parts[0], parts[1:]
    own, to_x, to_y, low, high = parts
    half = low.shape[0]
    from_x, from_y = swap(low, "seq", seq, 1), swap(high, "seq", seq, 2)
    to_x = jnp.concatenate([to_x[:half], to_x[half:] + from_y])
    to_y = jnp.concatenate([to_y[:half] + from_x, to_y[half:]])
    return own, [to_x, to_y]


def sum_kernel(count, dp, me_ref, *refs):
    parts, outs, held = refs[:count], refs[count:-1], refs[-1]
    held[...] = sum(part[...].astype(f32) for part in parts).astype(bf16)
    half = dp // 2
    for k in range(dp):
        outs[k // half][k % half] = held[jnp.bitwise_xor(me_ref[0], k)]


def near_parts(state, seq):
    own, sends = state
    return [own] + [swap(part, "seq", seq, 1 + step) for step, part in enumerate(sends)]


def sum_near(parts, dp, me):
    rows, width = parts[0].shape[1:]
    spec = pl.BlockSpec((dp, rows, COLUMNS), lambda i: (0, 0, i))
    out = pl.BlockSpec((dp // 2, rows, COLUMNS), lambda i: (0, 0, i))
    return pl.pallas_call(
        functools.partial(sum_kernel, len(parts), dp),
        out_shape=[jax.ShapeDtypeStruct((dp // 2, rows, width), bf16)] * 2,
        grid=(width // COLUMNS,),
        in_specs=[pl.BlockSpec(memory_space=pltpu.SMEM)] + [spec] * len(parts),
        out_specs=[out, out],
        scratch_shapes=[pltpu.VMEM((dp, rows, COLUMNS), bf16)],
        cost_estimate=pl.CostEstimate(
            flops=0, bytes_accessed=2 * (len(parts) + 1) * dp * rows * width, transcendentals=0
        ),
        compiler_params=pltpu.CompilerParams(vmem_limit_bytes=32 * 2**20),
    )(me, *parts)


def reduce_z(parts):
    total = sum(part.astype(f32) for part in parts).astype(bf16)
    return lax.psum_scatter(total, "dp", scatter_dimension=0)


def direct_z(state, dp):
    keep, send = state
    half = dp // 2
    rows = [keep[k] for k in range(half)] + [send[k] for k in range(half)]
    return sum(
        [rows[0].astype(f32)] + [swap(rows[k], "dp", dp, k).astype(f32) for k in range(1, dp)]
    )


def xor_onehot(count, rank):
    index = lax.broadcasted_iota(jnp.int32, (count, count), 0)
    other = lax.broadcasted_iota(jnp.int32, (count, count), 1)
    return (jnp.bitwise_xor(index, rank) == other).astype(f32)


def vectors_plane(shard, seq):
    found = jnp.stack([shard, swap(shard, "tensor", 2, 1)])
    return jnp.stack([found] + [swap(found, "seq", seq, k) for k in range(1, seq)])


def vectors_z(found, dp, rank):
    found = jnp.stack([found] + [swap(found, "dp", dp, k) for k in range(1, dp)])
    rows, width = found.shape[-2:]
    count = found.size // (rows * width)
    found = found.reshape(count, rows * width).astype(f32)
    placed = jnp.dot(xor_onehot(count, rank), found, precision=highest)
    return placed.reshape(count, rows, width).transpose(1, 0, 2).reshape(rows, count * width)


def sum_vectors_z(whole, sizes, rank):
    dp, seq = sizes
    rows, features = whole.shape
    count = dp * seq * 2
    width = features // count
    parts = whole.reshape(rows, count, width).transpose(1, 0, 2).reshape(count, rows * width)
    parts = jnp.dot(xor_onehot(count, rank), parts, precision=highest)
    parts = parts.reshape(dp, seq, 2, rows * width)
    total = parts[0]
    for step in range(1, dp):
        total = total + swap(parts[step], "dp", dp, step)
    return total


def sum_vectors_plane(parts, seq, rows):
    total = parts[0]
    for step in range(1, seq):
        total = total + swap(parts[step], "seq", seq, step)
    total = total[0] + swap(total[1], "tensor", 2, 1)
    return total.reshape(rows, -1)


def turn(operand, axis, size, rank):
    bit = 1
    shape = operand.shape
    while bit < size:
        split = operand.reshape(shape[:axis] + (size // (2 * bit), 2, bit) + shape[axis + 1 :])
        low, high = [lax.index_in_dim(split, at, axis + 1, keepdims=False) for at in (0, 1)]
        moved = jnp.bitwise_and(rank, bit) != 0
        both = [jnp.where(moved, high, low), jnp.where(moved, low, high)]
        operand = jnp.stack(both, axis=axis + 1).reshape(shape)
        bit *= 2
    return operand


def enter(first, second, seq, me):
    s, t = me[1], me[2]
    shapes = [member.shape for member in (first, second)]

    def pick(which):
        return jnp.concatenate(
            [
                lax.dynamic_index_in_dim(member, which, 0, keepdims=False).reshape(-1, shape[3])
                for member, shape in zip((first, second), shapes)
            ]
        )

    own, received = pick(t), swap(pick(1 - t), "tensor", 2, 1)
    rows, start = [], 0
    for shape in shapes:
        frames, places, features = shape[1:]
        stop = start + frames * places
        halves = [
            member[start:stop].reshape(frames, places, features) for member in (own, received)
        ]
        both = jnp.concatenate(halves, axis=1).reshape(frames, seq, -1, features)
        rows.append(turn(both, 1, seq, s).reshape(-1, features))
        start = stop
    return jnp.concatenate(rows)


def leave(tokens, shapes, seq, me):
    s, t = me[1], me[2]
    features = tokens.shape[1]
    own, other, start = [], [], 0
    for shape in shapes:
        frames, places = shape[1:3]
        stop = start + 2 * frames * places
        member = turn(tokens[start:stop].reshape(frames, seq, -1, features), 1, seq, s)
        member = member.reshape(frames, 2, places, features)
        own.append(member[:, 0].reshape(-1, features))
        other.append(member[:, 1].reshape(-1, features))
        start = stop
    own, received = jnp.concatenate(own), swap(jnp.concatenate(other), "tensor", 2, 1)
    results, start = [], 0
    for shape in shapes:
        frames, places = shape[1:3]
        stop = start + frames * places
        mine, theirs = own[start:stop], received[start:stop]
        both = jnp.stack([jnp.where(t == 0, mine, theirs), jnp.where(t == 0, theirs, mine)])
        results.append(both.reshape(shape))
        start = stop
    return results


def to_places(tokens, counts, seq):
    features = tokens.shape[1]
    members, start = [], 0
    for frames, places in counts:
        stop = start + frames * places
        members.append(tokens[start:stop].reshape(frames, seq, places // seq, features))
        start = stop
    pieces = [
        jnp.concatenate([member[:, step].reshape(-1, features) for member in members])
        for step in range(seq)
    ]
    pieces = jnp.stack(
        [pieces[0]] + [swap(pieces[step], "seq", seq, step) for step in range(1, seq)]
    )
    rows, start = [], 0
    for frames, places in counts:
        local = places // seq
        group = BLOCK // (frames * seq)
        stop = start + frames * local
        member = pieces[:, start:stop].reshape(seq, frames, local // group, group, features)
        rows.append(member.transpose(2, 0, 1, 3, 4).reshape(-1, features))
        start = stop
    return jnp.concatenate(rows)


def send_frames(tokens, counts, seq):
    features = tokens.shape[1]
    members, start = [], 0
    for frames, places in counts:
        local = places // seq
        group = BLOCK // (frames * seq)
        stop = start + seq * frames * local
        member = tokens[start:stop].reshape(local // group, seq, frames, group, features)
        members.append(member.transpose(1, 2, 0, 3, 4).reshape(seq, -1, features))
        start = stop
    pieces = jnp.concatenate(members, axis=1)
    return [pieces[0]] + [swap(pieces[step], "seq", seq, step) for step in range(1, seq)]


def join_frames(pieces, counts, seq):
    pieces = jnp.stack(pieces)
    features = pieces.shape[-1]
    rows, start = [], 0
    for frames, places in counts:
        local = places // seq
        stop = start + frames * local
        member = pieces[:, start:stop].reshape(seq, frames, local, features)
        rows.append(member.transpose(1, 0, 2, 3).reshape(-1, features))
        start = stop
    return jnp.concatenate(rows)


def allowed_bias(allowed):
    return jnp.where(allowed, 0.0, masked_score).astype(f32)


ROOT = 0.7978845608028654
CUBE = 0.044715


def ffn_kernel(n_ref, c_ref, up_ref, down_ref, z_ref, du_ref, mixed_ref, dn_ref):
    @pl.when(pl.program_id(0) == 0)
    def _():
        mixed_ref[...] = jnp.zeros_like(mixed_ref)
        dn_ref[...] = jnp.zeros_like(dn_ref)

    u = nn(n_ref[...], up_ref[...])
    da = nn(c_ref[...], down_ref[...])
    square = u * u
    bent = jnp.tanh(u * (ROOT + ROOT * CUBE * square))
    half = 0.5 + 0.5 * bent
    z = (u * half).astype(bf16)
    slope = half + (0.5 * u) * (1.0 - bent * bent) * (ROOT + 3.0 * ROOT * CUBE * square)
    du = (da * slope).astype(bf16)
    z_ref[...] = z
    du_ref[...] = du
    mixed_ref[...] += nt(z, down_ref[...])
    dn_ref[...] += nt(du, up_ref[...])


def ffn(normed, cotangent, pack):
    count, features = normed.shape
    hidden = pack.shape[1] // 2
    steps = hidden // COLUMNS
    rows = pl.BlockSpec((count, features), lambda i: (0, 0))
    units = pl.BlockSpec((count, COLUMNS), lambda i: (0, i))
    return pl.pallas_call(
        ffn_kernel,
        out_shape=[jax.ShapeDtypeStruct((count, hidden), bf16)] * 2
        + [jax.ShapeDtypeStruct((count, features), f32)] * 2,
        grid=(steps,),
        in_specs=[
            rows,
            rows,
            pl.BlockSpec((features, COLUMNS), lambda i: (0, i)),
            pl.BlockSpec((features, COLUMNS), lambda i: (0, i + steps)),
        ],
        out_specs=[units, units, rows, rows],
        cost_estimate=pl.CostEstimate(
            flops=8 * count * features * hidden,
            bytes_accessed=4 * features * hidden,
            transcendentals=count * hidden,
        ),
        compiler_params=pltpu.CompilerParams(vmem_limit_bytes=48 * 2**20),
    )(normed, cotangent, pack, pack)


def project(rows, half, stop):
    return jnp.dot(rows, half[:, :stop], preferred_element_type=f32).astype(bf16)


def project_out(mixed, halves, start):
    return sum(nt(member, half[:, start:]) for member, half in zip(mixed, halves))


def pull_out(gradient, half, start):
    return jnp.dot(gradient, half[:, start:], preferred_element_type=f32).astype(bf16)


def pull_in(packed, halves, stop):
    return sum(nt(member, half[:, :stop]) for member, half in zip(packed, halves))


def local(
    sizes,
    clips_a,
    actions_a,
    clips_b,
    actions_b,
    space_in,
    space_out,
    time_in,
    time_out,
    ffn_up,
    ffn_down,
    norm_gain,
    norm_shift,
    action_table,
    cot_a,
    cot_b,
):
    dp, seq = sizes
    me = [lax.axis_index(name) for name in ("dp", "seq", "tensor")]
    rank = (me[0] * seq + me[1]) * 2 + me[2]
    me_array = jnp.stack(me).astype(jnp.int32)
    rows_in, wide = space_in.shape[1], 3 * space_in.shape[2]

    def pack(inward, outward):
        slabs = inward.reshape(3, rows_in, -1, SLAB).transpose(1, 2, 0, 3)
        return jnp.concatenate([slabs.reshape(rows_in, wide), outward], axis=1)

    shapes = [clips_a.shape, clips_b.shape]
    frames = clips_a.shape[1]
    counts = [(shape[1], 2 * shape[2]) for shape in shapes]

    space_parts = parts_z(pack(space_in, space_out), dp)
    vectors = vectors_plane(jnp.concatenate([norm_gain, norm_shift, action_table]), seq)
    clips = enter(clips_a, clips_b, seq, me)
    cot = enter(cot_a, cot_b, seq, me)
    time_shard = pack(time_in, time_out)[None]
    ffn_shard = jnp.concatenate([ffn_up, ffn_down], axis=1)
    space_parts, vectors, clips, cot, time_shard, ffn_shard = phase(
        space_parts, vectors, clips, cot, time_shard, ffn_shard
    )
    space_block = jnp.stack(space_parts)
    vectors = vectors_z(vectors, dp, rank)
    space_near = spread_near(space_block, seq)
    time_block = lax.all_gather(time_shard[0], "dp", axis=0)

    gains, shifts, table = vectors[:3], vectors[3:6], vectors[6:]
    acts = jnp.concatenate(
        [
            lax.dynamic_index_in_dim(member, me[2], 0, keepdims=False)
            for member in (actions_a, actions_b)
        ]
    )
    onehot = (
        acts[:, None] == lax.broadcasted_iota(jnp.int32, (1, table.shape[0]), 1)
    ).astype(f32)
    rows_of = jnp.dot(onehot, table, precision=highest)
    spread = jnp.concatenate(
        [
            jnp.broadcast_to(
                rows_of[index * frames : (index + 1) * frames, None, :],
                (frames, places, table.shape[1]),
            ).reshape(-1, table.shape[1])
            for index, (_, places) in enumerate(counts)
        ]
    )
    entered = clips.astype(f32) + spread

    places_a, places_b = counts[0][1], counts[1][1]
    space_blocks = [(frame * places_a, places_a, False) for frame in range(frames)]
    space_blocks.append((frames * places_a, frames * places_b, True))
    index = lax.broadcasted_iota(jnp.int32, (frames * places_b, 1), 0) // places_b
    space_bias = allowed_bias(index == index.reshape(1, -1))
    total_tokens = clips.shape[0]
    time_blocks = [(start, BLOCK, True) for start in range(0, total_tokens, BLOCK)]
    group = BLOCK // (frames * seq)
    token = lax.broadcasted_iota(jnp.int32, (BLOCK, 1), 0)
    spot = token % group
    frame_id = (
        jnp.bitwise_xor(token // (frames * group), me[1]) * frames + (token // group) % frames
    )
    time_bias = allowed_bias(
        (spot == spot.reshape(1, -1)) & (frame_id.reshape(1, -1) <= frame_id)
    )

    masks = head_masks(max(BLOCK, places_a))

    normed_one = layer_norm(entered, gains[0], shifts[0])
    space_near, normed_one, entered = phase(space_near, normed_one, entered)
    space_far = spread_far(space_near, seq)
    space_far, space_near, time_block, ffn_shard = phase(
        space_far, space_near, time_block, ffn_shard
    )
    ffn_block = lax.all_gather(ffn_shard, "dp", axis=0)
    time_near = spread_near(time_block, seq)
    space_own = place(space_block, space_near, space_far, seq, me_array)
    space_other = swap(space_own, "tensor", 2, 1)
    packed_own = project(normed_one, space_own, wide)
    mixed_own = attend(packed_own, space_bias, masks, space_blocks)
    mixed_own, space_other = phase(mixed_own, space_other)
    space = [space_own, space_other]
    packed_one = [packed_own, project(normed_one, space[1], wide)]
    mixed_one = [mixed_own, attend(packed_one[1], space_bias, masks, space_blocks)]
    middle = (entered + project_out(mixed_one, space, wide)).astype(bf16)
    middle, time_near = phase(middle, time_near)
    middle = to_places(middle, counts, seq)
    time_far = spread_far(time_near, seq)
    middle, time_far, time_near, ffn_block = phase(middle, time_far, time_near, ffn_block)
    ffn_near = spread_near(ffn_block, seq)
    middle = middle.astype(f32)
    time_own = place(time_block, time_near, time_far, seq, me_array, False)
    time_other = swap(time_own, "tensor", 2, 1)
    normed_two = layer_norm(middle, gains[1], shifts[1])
    packed_own = project(normed_two, time_own, wide)
    mixed_own = attend(packed_own, time_bias, masks, time_blocks)
    mixed_own, time_other = phase(mixed_own, time_other)
    time = [time_own, time_other]
    packed_two = [packed_own, project(normed_two, time[1], wide)]
    mixed_two = [mixed_own, attend(packed_two[1], time_bias, masks, time_blocks)]
    before = middle + project_out(mixed_two, time, wide)
    normed_three = layer_norm(before, gains[2], shifts[2])
    ffn_near, normed_three, before = phase(ffn_near, normed_three, before)
    ffn_far = spread_far(ffn_near, seq)
    cot = to_places(cot, counts, seq)
    ffn_far, cot = phase(ffn_far, cot)
    ffn_own = place(ffn_block, ffn_near, ffn_far, seq, me_array, False)
    ffn_other = swap(ffn_own, "tensor", 2, 1)
    act_own, du_own, mixed_own, dn_own = ffn(normed_three, cot, ffn_own)
    act_own, ffn_other = phase(act_own, ffn_other)
    act_other, du_other, mixed_other, dn_other = ffn(normed_three, cot, ffn_other)
    mixed = (before + mixed_own + mixed_other).astype(bf16)
    mixed, act_other, du_other, dn_other = phase(mixed, act_other, du_other, dn_other)
    mixed = send_frames(mixed, counts, seq)
    down_other = swap(grad_other([cot], [act_other]), "tensor", 2, 1)
    up_other = grad_other([normed_three], [du_other])
    d_input, gain_three, shift_three = norm_back(before, gains[2], dn_own + dn_other)
    gradient = cot.astype(f32) + d_input
    rounded = gradient.astype(bf16)
    down_other, up_other, rounded = phase(down_other, up_other, rounded)
    up_other = swap(up_other, "tensor", 2, 1)
    down_grads = grad_parts([cot], [act_own], down_other, sizes, me_array)
    upstream = [pull_out(rounded, half, wide) for half in time]
    down_grads, upstream, up_other, mixed = phase(down_grads, upstream, up_other, mixed)
    down_state = reduce_far(down_grads, seq)
    up_grads = grad_parts([normed_three], [du_own], up_other, sizes, me_array)
    d_own = attend_back(packed_two[0], upstream[0], time_bias, masks, time_blocks)
    up_grads, d_own, upstream, down_state = phase(up_grads, d_own, upstream, down_state)
    down_near = near_parts(down_state, seq)
    d_other = attend_back(packed_two[1], upstream[1], time_bias, masks, time_blocks)
    d_packed = [d_own, d_other]
    d_input, gain_two, shift_two = norm_back(middle, gains[1], pull_in(d_packed, time, wide))
    rounded_two = (gradient + d_input).astype(bf16)
    rounded_two, d_packed, down_near = phase(rounded_two, d_packed, down_near)
    rounded_two = join_frames(send_frames(rounded_two, counts, seq), counts, seq)
    left = [normed_two, rounded]
    time_other = swap(grad_other(left, [d_packed[1], mixed_two[1]]), "tensor", 2, 1)
    mixed = leave(join_frames(mixed, counts, seq), shapes, seq, me)
    rounded, time_other, mixed = phase(rounded_two, time_other, mixed)
    up_state = reduce_far(up_grads, seq)
    grad_down = reduce_z(down_near)
    time_grads = grad_parts(left, [d_packed[0], mixed_two[0]], time_other, sizes, me_array)
    upstream = [pull_out(rounded, half, wide) for half in space]
    time_grads, upstream, up_state = phase(time_grads, upstream, up_state)
    up_near = near_parts(up_state, seq)
    time_state = reduce_far(time_grads, seq)
    d_other = attend_back(packed_one[1], upstream[1], space_bias, masks, space_blocks)
    left = [normed_one, rounded]
    space_other = swap(grad_other(left, [d_other, mixed_one[1]]), "tensor", 2, 1)
    d_own = attend_back(packed_one[0], upstream[0], space_bias, masks, space_blocks)
    d_own, d_other, up_near, time_state, space_other = phase(
        d_own, d_other, up_near, time_state, space_other
    )
    time_near = near_parts(time_state, seq)
    space_grads = grad_parts(left, [d_own, mixed_one[0]], space_other, sizes, me_array)
    space_state = reduce_far(space_grads, seq)
    grad_up = reduce_z(up_near)
    d_normed = pull_in([d_own, d_other], space, wide)
    d_input, gain_one, shift_one = norm_back(entered, gains[0], d_normed)
    gradient = rounded.astype(f32) + d_input
    time_near, space_state, gradient, grad_down = phase(
        time_near, space_state, gradient, grad_down
    )
    space_near = near_parts(space_state, seq)
    grad_time = reduce_z(time_near)
    sums, start = [], 0
    for frame_count, places in counts:
        stop = start + frame_count * places
        sums.append(jnp.sum(gradient[start:stop].reshape(frame_count, places, -1), axis=1))
        start = stop
    grad_table = jnp.dot(onehot.T, jnp.concatenate(sums), precision=highest)
    vector_grads = jnp.concatenate(
        [
            jnp.stack([gain_one, gain_two, gain_three, shift_one, shift_two, shift_three]),
            grad_table,
        ]
    )
    rows = vector_grads.shape[0]
    vector_grads = sum_vectors_z(vector_grads, sizes, rank)
    grads = leave(gradient.astype(bf16), shapes, seq, me)
    space_near, grads, vector_grads, grad_up = phase(space_near, grads, vector_grads, grad_up)
    vector_grads = sum_vectors_plane(vector_grads, seq, rows)
    grad_space = direct_z(sum_near(space_near, dp, me_array), dp)

    def unpack(member):
        slabs = member[:, :wide].reshape(rows_in, -1, 3, SLAB)
        return slabs.transpose(2, 0, 1, 3).reshape(3, rows_in, -1)

    return (
        *mixed,
        *grads,
        unpack(grad_space),
        grad_space[:, wide:],
        unpack(grad_time.astype(f32)),
        grad_time[:, wide:].astype(f32),
        grad_up.astype(f32),
        grad_down.astype(f32),
        vector_grads[:3],
        vector_grads[3:6],
        vector_grads[6:],
    )


def solution(mesh):
    sizes = (mesh.shape["dp"], mesh.shape["seq"])
    in_specs = (
        P("dp", "seq", "tensor", None),
        P("dp", "seq"),
        P("dp", "seq", "tensor", None),
        P("dp", "seq"),
        P(None, ("dp", "seq"), "tensor"),
        P(("dp", "seq"), "tensor"),
        P(None, ("dp", "seq"), "tensor"),
        P(("dp", "seq"), "tensor"),
        P(("dp", "seq"), "tensor"),
        P(("dp", "seq"), "tensor"),
        P(None, ("dp", "seq", "tensor")),
        P(None, ("dp", "seq", "tensor")),
        P(None, ("dp", "seq", "tensor")),
        P("dp", "seq", "tensor", None),
        P("dp", "seq", "tensor", None),
    )
    out_specs = (
        P("dp", "seq", "tensor", None),
        P("dp", "seq", "tensor", None),
        P("dp", "seq", "tensor", None),
        P("dp", "seq", "tensor", None),
        P(None, ("dp", "seq"), "tensor"),
        P(("dp", "seq"), "tensor"),
        P(None, ("dp", "seq"), "tensor"),
        P(("dp", "seq"), "tensor"),
        P(("dp", "seq"), "tensor"),
        P(("dp", "seq"), "tensor"),
        P(None, ("dp", "seq", "tensor")),
        P(None, ("dp", "seq", "tensor")),
        P(None, ("dp", "seq", "tensor")),
    )
    return jax.shard_map(
        functools.partial(local, sizes),
        mesh=mesh,
        in_specs=in_specs,
        out_specs=out_specs,
        check_vma=False,
    )
```

```python
import functools

import jax
import jax.numpy as jnp
from jax import lax
from jax.experimental import pallas as pl
from jax.experimental.pallas import tpu as pltpu
from jax.sharding import PartitionSpec as P

HDIM = 64
BLOCK = 128

epsilon = 1e-05
masked_score = -1e30
highest = lax.Precision.HIGHEST
bf16 = jnp.bfloat16
f32 = jnp.float32


def swap(operand, axis, size, step):
    return lax.ppermute(operand, axis, [(i, i ^ step) for i in range(size)])


def norm_stats(operand):
    centred = operand - jnp.mean(operand, axis=-1, keepdims=True)
    inverse = lax.rsqrt(jnp.mean(centred * centred, axis=-1, keepdims=True) + epsilon)
    return centred * inverse, inverse


def layer_norm(operand, gain_row, shift_row):
    standard, _ = norm_stats(operand)
    return (standard * gain_row + shift_row).astype(bf16)


def norm_back(operand, gain_row, upstream):
    standard, inverse = norm_stats(operand)
    scaled = upstream * gain_row
    inner = (
        scaled
        - jnp.mean(scaled, axis=-1, keepdims=True)
        - standard * jnp.mean(scaled * standard, axis=-1, keepdims=True)
    )
    return inverse * inner, jnp.sum(upstream * standard, axis=0), jnp.sum(upstream, axis=0)


SLAB = 2 * HDIM


def small_cost():
    return pl.CostEstimate(flops=1024, bytes_accessed=1024, transcendentals=0)


def nt(left, right):
    return lax.dot_general(left, right, (((1,), (1,)), ((), ())), preferred_element_type=f32)


def nn(left, right):
    return lax.dot_general(left, right, (((1,), (0,)), ((), ())), preferred_element_type=f32)


def tn(left, right):
    return lax.dot_general(left, right, (((0,), (0,)), ((), ())), preferred_element_type=f32)


def soft_weights(scores):
    shifted = jnp.exp(scores - jnp.max(scores, axis=-1, keepdims=True))
    return shifted * (1.0 / jnp.sum(shifted, axis=-1, keepdims=True))


def attend_kernel(blocks, bias_ref, mask_ref, p_ref, o_ref):
    items = [(start, size, masked, head) for start, size, masked in blocks for head in (0, 1)]
    scores = []
    for start, size, masked, head in items:
        rows = pl.ds(start, size)
        part = nt(p_ref[rows, :SLAB] * mask_ref[head, :size, :], p_ref[rows, SLAB : 2 * SLAB])
        scores.append(part + bias_ref[...] if masked else part)
    weights = [soft_weights(part).astype(bf16) for part in scores]
    parts = [
        nn(part, p_ref[pl.ds(start, size), 2 * SLAB :] * mask_ref[2 + head, :size, :])
        for part, (start, size, _, head) in zip(weights, items)
    ]
    for at, (start, size, _) in enumerate(blocks):
        o_ref[pl.ds(start, size), :] = (parts[2 * at] + parts[2 * at + 1]).astype(bf16)


def attend_back_kernel(blocks, bias_ref, mask_ref, p_ref, d_ref, o_ref):
    items = [(start, size, masked, head) for start, size, masked in blocks for head in (0, 1)]
    scores, d_weights = [], []
    for start, size, masked, head in items:
        rows = pl.ds(start, size)
        part = nt(p_ref[rows, :SLAB] * mask_ref[head, :size, :], p_ref[rows, SLAB : 2 * SLAB])
        scores.append(part + bias_ref[...] if masked else part)
        d_weights.append(nt(d_ref[rows, :] * mask_ref[2 + head, :size, :], p_ref[rows, 2 * SLAB :]))
    weights = [soft_weights(part) for part in scores]
    d_scores = [
        (part * (grad - jnp.sum(part * grad, axis=-1, keepdims=True))).astype(bf16)
        for part, grad in zip(weights, d_weights)
    ]
    weights = [part.astype(bf16) for part in weights]
    for index, (start, size, _) in enumerate(blocks):
        rows = pl.ds(start, size)
        dq, dk, dv = 0.0, 0.0, 0.0
        for head in (0, 1):
            scaled, whole = mask_ref[head, :size, :], mask_ref[2 + head, :size, :]
            d_score, weight = d_scores[2 * index + head], weights[2 * index + head]
            dq += nn(d_score, p_ref[rows, SLAB : 2 * SLAB] * scaled)
            dk += tn(d_score, p_ref[rows, :SLAB] * scaled)
            dv += tn(weight, d_ref[rows, :] * whole)
        o_ref[rows, :SLAB] = dq.astype(bf16)
        o_ref[rows, SLAB : 2 * SLAB] = dk.astype(bf16)
        o_ref[rows, 2 * SLAB :] = dv.astype(bf16)


def head_masks(rows):
    low = lax.broadcasted_iota(jnp.int32, (rows, SLAB), 1) < HDIM
    masks = jnp.stack([low, ~low]).astype(bf16)
    return jnp.concatenate([masks * (HDIM**-0.5), masks])


def slab_spec(count, width):
    return pl.BlockSpec((count, width), lambda i: (0, i))


def attend_specs(packed, bias, masks, blocks, products):
    count, width = packed.shape
    slabs = width // (3 * SLAB)
    specs = [
        pl.BlockSpec(bias.shape, lambda i: (0, 0)),
        pl.BlockSpec(masks.shape, lambda i: (0, 0, 0)),
        slab_spec(count, 3 * SLAB),
    ]
    scores = 2 * slabs * sum(size * size for _, size, _ in blocks)
    cost = pl.CostEstimate(
        flops=2 * products * scores * SLAB,
        bytes_accessed=count * width * products,
        transcendentals=scores,
    )
    return count, slabs, specs, cost


def attend(packed, bias, masks, blocks):
    count, slabs, specs, cost = attend_specs(packed, bias, masks, blocks, 2)
    return pl.pallas_call(
        functools.partial(attend_kernel, blocks),
        out_shape=jax.ShapeDtypeStruct((count, slabs * SLAB), bf16),
        grid=(slabs,),
        in_specs=specs,
        out_specs=slab_spec(count, SLAB),
        cost_estimate=cost,
        compiler_params=pltpu.CompilerParams(vmem_limit_bytes=32 * 2**20),
    )(bias, masks, packed)


def attend_back(packed, upstream, bias, masks, blocks):
    count, slabs, specs, cost = attend_specs(packed, bias, masks, blocks, 5)
    return pl.pallas_call(
        functools.partial(attend_back_kernel, blocks),
        out_shape=jax.ShapeDtypeStruct(packed.shape, bf16),
        grid=(slabs,),
        in_specs=[*specs, slab_spec(count, SLAB)],
        out_specs=slab_spec(count, 3 * SLAB),
        cost_estimate=cost,
        compiler_params=pltpu.CompilerParams(vmem_limit_bytes=32 * 2**20),
    )(bias, masks, packed, upstream)


def place_kernel(order, count, relative, me_ref, *refs):
    pieces, out_ref = refs[:count], refs[count]
    for piece, row, kz, ks in order:
        at_z = jnp.bitwise_xor(me_ref[0], kz) if relative else kz
        at = at_z, jnp.bitwise_xor(me_ref[1], ks)
        out_ref[at] = pieces[piece][row]


def phase(*state):
    return lax.optimization_barrier(state)


def double_z(state, step, dp):
    return jnp.concatenate([state, swap(state, "dp", dp, step)])


def parts_z(shard, dp):
    return [shard] + [swap(shard, "dp", dp, k) for k in range(1, dp)]


def spread_z(state, step, dp):
    while step < dp:
        state = double_z(state, step, dp)
        step *= 2
    return state


def spread_near(block, seq):
    if seq == 4:
        return [swap(block, "seq", seq, 1), swap(block, "seq", seq, 2)]
    return [swap(block, "seq", seq, step) for step in range(1, seq)]


def spread_far(near, seq):
    if seq != 4:
        return []
    from_x, from_y = near
    half = from_x.shape[0] // 2
    return [swap(from_y[:half], "seq", seq, 1), swap(from_x[half:], "seq", seq, 2)]


def place(block, near, far, seq, me, relative=True):
    dp, rows, width = block.shape
    half = dp // 2
    pieces = [block, *near, *far]
    order = [(index, k, k, index) for index in range(1 + len(near)) for k in range(dp)]
    if far:
        order += [(3, k, k, 3) for k in range(half)]
        order += [(4, k - half, k, 3) for k in range(half, dp)]
    whole = pl.pallas_call(
        functools.partial(place_kernel, order, len(pieces), relative),
        out_shape=jax.ShapeDtypeStruct((dp, seq, rows, width), block.dtype),
        grid=(width // COLUMNS,),
        in_specs=[pl.BlockSpec(memory_space=pltpu.SMEM)]
        + [
            pl.BlockSpec((piece.shape[0], rows, COLUMNS), lambda i: (0, 0, i)) for piece in pieces
        ],
        out_specs=pl.BlockSpec((dp, seq, rows, COLUMNS), lambda i: (0, 0, 0, i)),
        cost_estimate=pl.CostEstimate(
            flops=0, bytes_accessed=4 * dp * seq * rows * width, transcendentals=0
        ),
        compiler_params=pltpu.CompilerParams(vmem_limit_bytes=32 * 2**20),
    )(me, *pieces)
    return whole.reshape(dp * seq * rows, width)


def each_block(pairs, splits, left, right, store):
    at = pl.program_id(0)
    if pairs == 1:
        store(tn(left[0][...], right[0][...]))
        return
    for pair in range(pairs):

        @pl.when((at >= splits[pair]) & (at < splits[pair + 1]))
        def _():
            store(tn(left[pair][...], right[pair][...]))


def grad_kernel(pairs, splits, *refs):
    left, right, out_ref = refs[:pairs], refs[pairs : 2 * pairs], refs[-1]

    def store(total):
        out_ref[...] = total.astype(bf16)

    each_block(pairs, splits, left, right, store)


def grad_parts_kernel(pairs, splits, dp, seq, me_ref, *refs):
    left, right, other_ref = refs[:pairs], refs[pairs : 2 * pairs], refs[2 * pairs]
    outs, held = refs[2 * pairs + 1 : -1], refs[-1]
    rows = other_ref.shape[0] // (dp * seq)

    def store(total):
        total = total + other_ref[...].astype(f32)
        held[...] = total.astype(bf16).reshape(held.shape)

    each_block(pairs, splits, left, right, store)
    for k in range(seq):
        owner = jnp.bitwise_xor(me_ref[1], k)
        for z in range(dp):
            part = held[z * seq + owner]
            if seq == 4 and k == 3:
                outs[3 + z // (dp // 2)][z % (dp // 2)] = part
            else:
                outs[k][z] = part


COLUMNS = 512


def grad_specs(left, right):
    rows, features = left[0].shape
    splits = [0]
    for member in right:
        splits.append(splits[-1] + member.shape[1] // COLUMNS)
    specs = [pl.BlockSpec(member.shape, lambda i: (0, 0)) for member in left]

    def columns(first, last):
        return lambda i: (0, jnp.clip(i - first, 0, last - first - 1))

    for first, last in zip(splits, splits[1:]):
        specs.append(pl.BlockSpec((rows, COLUMNS), columns(first, last)))
    width = splits[-1] * COLUMNS
    cost = pl.CostEstimate(
        flops=2 * rows * features * width,
        bytes_accessed=4 * width * features,
        transcendentals=0,
    )
    return splits, specs, width, cost


def grad_other(left, right):
    splits, specs, width, cost = grad_specs(left, right)
    features = left[0].shape[1]
    return pl.pallas_call(
        functools.partial(grad_kernel, len(left), splits),
        out_shape=jax.ShapeDtypeStruct((features, width), bf16),
        grid=(width // COLUMNS,),
        in_specs=specs,
        out_specs=pl.BlockSpec((features, COLUMNS), lambda i: (0, i)),
        cost_estimate=small_cost(),
        compiler_params=pltpu.CompilerParams(vmem_limit_bytes=32 * 2**20),
    )(*left, *right)


def grad_parts(left, right, other, sizes, me):
    dp, seq = sizes
    splits, specs, width, cost = grad_specs(left, right)
    features = left[0].shape[1]
    rows = features // (dp * seq)
    depths = [dp] * seq if seq != 4 else [dp, dp, dp, dp // 2, dp - dp // 2]
    return pl.pallas_call(
        functools.partial(grad_parts_kernel, len(left), splits, dp, seq),
        out_shape=[jax.ShapeDtypeStruct((depth, rows, width), bf16) for depth in depths],
        grid=(width // COLUMNS,),
        in_specs=[
            pl.BlockSpec(memory_space=pltpu.SMEM),
            *specs,
            pl.BlockSpec((features, COLUMNS), lambda i: (0, i)),
        ],
        out_specs=[pl.BlockSpec((depth, rows, COLUMNS), lambda i: (0, 0, i)) for depth in depths],
        scratch_shapes=[pltpu.VMEM((dp * seq, rows, COLUMNS), bf16)],
        cost_estimate=cost,
        compiler_params=pltpu.CompilerParams(vmem_limit_bytes=40 * 2**20),
    )(me, *left, *right, other)


def reduce_far(parts, seq):
    if seq != 4:
        return parts[0], parts[1:]
    own, to_x, to_y, low, high = parts
    half = low.shape[0]
    from_x, from_y = swap(low, "seq", seq, 1), swap(high, "seq", seq, 2)
    to_x = jnp.concatenate([to_x[:half], to_x[half:] + from_y])
    to_y = jnp.concatenate([to_y[:half] + from_x, to_y[half:]])
    return own, [to_x, to_y]


def sum_kernel(count, dp, me_ref, *refs):
    parts, outs, held = refs[:count], refs[count:-1], refs[-1]
    held[...] = sum(part[...].astype(f32) for part in parts).astype(bf16)
    half = dp // 2
    for k in range(dp):
        outs[k // half][k % half] = held[jnp.bitwise_xor(me_ref[0], k)]


def near_parts(state, seq):
    own, sends = state
    return [own] + [swap(part, "seq", seq, 1 + step) for step, part in enumerate(sends)]


def sum_near(parts, dp, me):
    rows, width = parts[0].shape[1:]
    spec = pl.BlockSpec((dp, rows, COLUMNS), lambda i: (0, 0, i))
    out = pl.BlockSpec((dp // 2, rows, COLUMNS), lambda i: (0, 0, i))
    return pl.pallas_call(
        functools.partial(sum_kernel, len(parts), dp),
        out_shape=[jax.ShapeDtypeStruct((dp // 2, rows, width), bf16)] * 2,
        grid=(width // COLUMNS,),
        in_specs=[pl.BlockSpec(memory_space=pltpu.SMEM)] + [spec] * len(parts),
        out_specs=[out, out],
        scratch_shapes=[pltpu.VMEM((dp, rows, COLUMNS), bf16)],
        cost_estimate=pl.CostEstimate(
            flops=0, bytes_accessed=2 * (len(parts) + 1) * dp * rows * width, transcendentals=0
        ),
        compiler_params=pltpu.CompilerParams(vmem_limit_bytes=32 * 2**20),
    )(me, *parts)


def reduce_z(parts):
    total = sum(part.astype(f32) for part in parts).astype(bf16)
    return lax.psum_scatter(total, "dp", scatter_dimension=0)


def direct_z(state, dp):
    keep, send = state
    half = dp // 2
    rows = [keep[k] for k in range(half)] + [send[k] for k in range(half)]
    return sum(
        [rows[0].astype(f32)] + [swap(rows[k], "dp", dp, k).astype(f32) for k in range(1, dp)]
    )


def xor_onehot(count, rank):
    index = lax.broadcasted_iota(jnp.int32, (count, count), 0)
    other = lax.broadcasted_iota(jnp.int32, (count, count), 1)
    return (jnp.bitwise_xor(index, rank) == other).astype(f32)


def vectors_plane(shard, seq):
    found = jnp.stack([shard, swap(shard, "tensor", 2, 1)])
    return jnp.stack([found] + [swap(found, "seq", seq, k) for k in range(1, seq)])


def vectors_z(found, dp, rank):
    found = jnp.stack([found] + [swap(found, "dp", dp, k) for k in range(1, dp)])
    rows, width = found.shape[-2:]
    count = found.size // (rows * width)
    found = found.reshape(count, rows * width).astype(f32)
    placed = jnp.dot(xor_onehot(count, rank), found, precision=highest)
    return placed.reshape(count, rows, width).transpose(1, 0, 2).reshape(rows, count * width)


def vector_parts(whole, sizes, rank):
    dp, seq = sizes
    rows, features = whole.shape
    count = dp * seq * 2
    width = features // count
    parts = whole.reshape(rows, count, width).transpose(1, 0, 2).reshape(count, rows * width)
    parts = jnp.dot(xor_onehot(count, rank), parts, precision=highest)
    return parts.reshape(dp, seq, 2, rows * width)


def sum_vectors_z(parts, dp):
    total = parts[0]
    for step in range(1, dp):
        total = total + swap(parts[step], "dp", dp, step)
    return total


def sum_vectors_plane(parts, seq, rows):
    total = parts[0]
    for step in range(1, seq):
        total = total + swap(parts[step], "seq", seq, step)
    total = total[0] + swap(total[1], "tensor", 2, 1)
    return total.reshape(rows, -1)


def turn(operand, axis, size, rank):
    bit = 1
    shape = operand.shape
    while bit < size:
        split = operand.reshape(shape[:axis] + (size // (2 * bit), 2, bit) + shape[axis + 1 :])
        low, high = [lax.index_in_dim(split, at, axis + 1, keepdims=False) for at in (0, 1)]
        moved = jnp.bitwise_and(rank, bit) != 0
        both = [jnp.where(moved, high, low), jnp.where(moved, low, high)]
        operand = jnp.stack(both, axis=axis + 1).reshape(shape)
        bit *= 2
    return operand


def enter(first, second, seq, me):
    s, t = me[1], me[2]
    shapes = [member.shape for member in (first, second)]

    def pick(which):
        return jnp.concatenate(
            [
                lax.dynamic_index_in_dim(member, which, 0, keepdims=False).reshape(-1, shape[3])
                for member, shape in zip((first, second), shapes)
            ]
        )

    own, received = pick(t), swap(pick(1 - t), "tensor", 2, 1)
    rows, start = [], 0
    for shape in shapes:
        frames, places, features = shape[1:]
        stop = start + frames * places
        halves = [
            member[start:stop].reshape(frames, places, features) for member in (own, received)
        ]
        both = jnp.concatenate(halves, axis=1).reshape(frames, seq, -1, features)
        rows.append(turn(both, 1, seq, s).reshape(-1, features))
        start = stop
    return jnp.concatenate(rows)


def leave(tokens, shapes, seq, me):
    s, t = me[1], me[2]
    features = tokens.shape[1]
    own, other, start = [], [], 0
    for shape in shapes:
        frames, places = shape[1:3]
        stop = start + 2 * frames * places
        member = turn(tokens[start:stop].reshape(frames, seq, -1, features), 1, seq, s)
        member = member.reshape(frames, 2, places, features)
        own.append(member[:, 0].reshape(-1, features))
        other.append(member[:, 1].reshape(-1, features))
        start = stop
    own, received = jnp.concatenate(own), swap(jnp.concatenate(other), "tensor", 2, 1)
    results, start = [], 0
    for shape in shapes:
        frames, places = shape[1:3]
        stop = start + frames * places
        mine, theirs = own[start:stop], received[start:stop]
        both = jnp.stack([jnp.where(t == 0, mine, theirs), jnp.where(t == 0, theirs, mine)])
        results.append(both.reshape(shape))
        start = stop
    return results


def to_places(tokens, counts, seq):
    features = tokens.shape[1]
    members, start = [], 0
    for frames, places in counts:
        stop = start + frames * places
        members.append(tokens[start:stop].reshape(frames, seq, places // seq, features))
        start = stop
    pieces = [
        jnp.concatenate([member[:, step].reshape(-1, features) for member in members])
        for step in range(seq)
    ]
    pieces = jnp.stack(
        [pieces[0]] + [swap(pieces[step], "seq", seq, step) for step in range(1, seq)]
    )
    rows, start = [], 0
    for frames, places in counts:
        local = places // seq
        group = BLOCK // (frames * seq)
        stop = start + frames * local
        member = pieces[:, start:stop].reshape(seq, frames, local // group, group, features)
        rows.append(member.transpose(2, 0, 1, 3, 4).reshape(-1, features))
        start = stop
    return jnp.concatenate(rows)


def send_frames(tokens, counts, seq):
    features = tokens.shape[1]
    members, start = [], 0
    for frames, places in counts:
        local = places // seq
        group = BLOCK // (frames * seq)
        stop = start + seq * frames * local
        member = tokens[start:stop].reshape(local // group, seq, frames, group, features)
        members.append(member.transpose(1, 2, 0, 3, 4).reshape(seq, -1, features))
        start = stop
    pieces = jnp.concatenate(members, axis=1)
    return [pieces[0]] + [swap(pieces[step], "seq", seq, step) for step in range(1, seq)]


def join_frames(pieces, counts, seq):
    pieces = jnp.stack(pieces)
    features = pieces.shape[-1]
    rows, start = [], 0
    for frames, places in counts:
        local = places // seq
        stop = start + frames * local
        member = pieces[:, start:stop].reshape(seq, frames, local, features)
        rows.append(member.transpose(1, 0, 2, 3).reshape(-1, features))
        start = stop
    return jnp.concatenate(rows)


def allowed_bias(allowed):
    return jnp.where(allowed, 0.0, masked_score).astype(f32)


ROOT = 0.7978845608028654
CUBE = 0.044715


def ffn_kernel(n_ref, c_ref, up_ref, down_ref, z_ref, du_ref, mixed_ref, dn_ref):
    @pl.when(pl.program_id(0) == 0)
    def _():
        mixed_ref[...] = jnp.zeros_like(mixed_ref)
        dn_ref[...] = jnp.zeros_like(dn_ref)

    u = nn(n_ref[...], up_ref[...])
    da = nn(c_ref[...], down_ref[...])
    square = u * u
    bent = jnp.tanh(u * (ROOT + ROOT * CUBE * square))
    half = 0.5 + 0.5 * bent
    z = (u * half).astype(bf16)
    slope = half + (0.5 * u) * (1.0 - bent * bent) * (ROOT + 3.0 * ROOT * CUBE * square)
    du = (da * slope).astype(bf16)
    z_ref[...] = z
    du_ref[...] = du
    mixed_ref[...] += nt(z, down_ref[...])
    dn_ref[...] += nt(du, up_ref[...])


def ffn(normed, cotangent, pack):
    count, features = normed.shape
    hidden = pack.shape[1] // 2
    steps = hidden // COLUMNS
    rows = pl.BlockSpec((count, features), lambda i: (0, 0))
    units = pl.BlockSpec((count, COLUMNS), lambda i: (0, i))
    return pl.pallas_call(
        ffn_kernel,
        out_shape=[jax.ShapeDtypeStruct((count, hidden), bf16)] * 2
        + [jax.ShapeDtypeStruct((count, features), f32)] * 2,
        grid=(steps,),
        in_specs=[
            rows,
            rows,
            pl.BlockSpec((features, COLUMNS), lambda i: (0, i)),
            pl.BlockSpec((features, COLUMNS), lambda i: (0, i + steps)),
        ],
        out_specs=[units, units, rows, rows],
        cost_estimate=pl.CostEstimate(
            flops=8 * count * features * hidden,
            bytes_accessed=4 * features * hidden,
            transcendentals=count * hidden,
        ),
        compiler_params=pltpu.CompilerParams(vmem_limit_bytes=48 * 2**20),
    )(normed, cotangent, pack, pack)


def project(rows, half, stop):
    return jnp.dot(rows, half[:, :stop], preferred_element_type=f32).astype(bf16)


def project_out(mixed, halves, start):
    return sum(nt(member, half[:, start:]) for member, half in zip(mixed, halves))


def pull_out(gradient, half, start):
    return jnp.dot(gradient, half[:, start:], preferred_element_type=f32).astype(bf16)


def pull_in_kernel(own_ref, other_ref, own_half_ref, other_half_ref, o_ref):
    o_ref[...] = nt(own_ref[...], own_half_ref[...]) + nt(other_ref[...], other_half_ref[...])


def pull_in(packed, halves, stop):
    count = packed[0].shape[0]
    features = halves[0].shape[0]
    columns_of = 2 * SLAB
    rows = pl.BlockSpec((count, stop), lambda i: (0, 0))
    half = pl.BlockSpec((columns_of, stop), lambda i: (i, 0))
    return pl.pallas_call(
        pull_in_kernel,
        out_shape=jax.ShapeDtypeStruct((count, features), f32),
        grid=(features // columns_of,),
        in_specs=[rows, rows, half, half],
        out_specs=pl.BlockSpec((count, columns_of), lambda i: (0, i)),
        cost_estimate=small_cost(),
        compiler_params=pltpu.CompilerParams(vmem_limit_bytes=32 * 2**20),
    )(*packed, *halves)


def local(
    sizes,
    clips_a,
    actions_a,
    clips_b,
    actions_b,
    space_in,
    space_out,
    time_in,
    time_out,
    ffn_up,
    ffn_down,
    norm_gain,
    norm_shift,
    action_table,
    cot_a,
    cot_b,
):
    dp, seq = sizes
    me = [lax.axis_index(name) for name in ("dp", "seq", "tensor")]
    rank = (me[0] * seq + me[1]) * 2 + me[2]
    me_array = jnp.stack(me).astype(jnp.int32)
    rows_in, wide = space_in.shape[1], 3 * space_in.shape[2]

    def pack(inward, outward):
        slabs = inward.reshape(3, rows_in, -1, SLAB).transpose(1, 2, 0, 3)
        return jnp.concatenate([slabs.reshape(rows_in, wide), outward], axis=1)

    shapes = [clips_a.shape, clips_b.shape]
    frames = clips_a.shape[1]
    counts = [(shape[1], 2 * shape[2]) for shape in shapes]

    space_block = lax.all_gather(pack(space_in, space_out), "dp", axis=0)
    vectors = vectors_plane(jnp.concatenate([norm_gain, norm_shift, action_table]), seq)
    cot = to_places(enter(cot_a, cot_b, seq, me), counts, seq)
    clips = enter(clips_a, clips_b, seq, me)
    time_shard = pack(time_in, time_out)[None]
    ffn_shard = jnp.concatenate([ffn_up, ffn_down], axis=1)
    space_block, vectors, clips, cot, time_shard, ffn_shard = phase(
        space_block, vectors, clips, cot, time_shard, ffn_shard
    )
    vectors = vectors_z(vectors, dp, rank)
    space_near = spread_near(space_block, seq)
    time_block = lax.all_gather(time_shard[0], "dp", axis=0)

    gains, shifts, table = vectors[:3], vectors[3:6], vectors[6:]
    acts = jnp.concatenate(
        [
            lax.dynamic_index_in_dim(member, me[2], 0, keepdims=False)
            for member in (actions_a, actions_b)
        ]
    )
    onehot = (
        acts[:, None] == lax.broadcasted_iota(jnp.int32, (1, table.shape[0]), 1)
    ).astype(f32)
    rows_of = jnp.dot(onehot, table, precision=highest)
    spread = jnp.concatenate(
        [
            jnp.broadcast_to(
                rows_of[index * frames : (index + 1) * frames, None, :],
                (frames, places, table.shape[1]),
            ).reshape(-1, table.shape[1])
            for index, (_, places) in enumerate(counts)
        ]
    )
    entered = clips.astype(f32) + spread

    places_a, places_b = counts[0][1], counts[1][1]
    space_blocks = [(frame * places_a, places_a, False) for frame in range(frames)]
    space_blocks.append((frames * places_a, frames * places_b, True))
    index = lax.broadcasted_iota(jnp.int32, (frames * places_b, 1), 0) // places_b
    space_bias = allowed_bias(index == index.reshape(1, -1))
    total_tokens = clips.shape[0]
    time_blocks = [(start, BLOCK, True) for start in range(0, total_tokens, BLOCK)]
    group = BLOCK // (frames * seq)
    token = lax.broadcasted_iota(jnp.int32, (BLOCK, 1), 0)
    spot = token % group
    frame_id = (
        jnp.bitwise_xor(token // (frames * group), me[1]) * frames + (token // group) % frames
    )
    time_bias = allowed_bias(
        (spot == spot.reshape(1, -1)) & (frame_id.reshape(1, -1) <= frame_id)
    )

    masks = head_masks(max(BLOCK, places_a))

    normed_one = layer_norm(entered, gains[0], shifts[0])
    space_near, normed_one, entered = phase(space_near, normed_one, entered)
    space_far = spread_far(space_near, seq)
    space_far, space_near, time_block, ffn_shard = phase(
        space_far, space_near, time_block, ffn_shard
    )
    ffn_block = lax.all_gather(ffn_shard, "dp", axis=0)
    time_near = spread_near(time_block, seq)
    space_own = place(space_block, space_near, space_far, seq, me_array, False)
    space_other = swap(space_own, "tensor", 2, 1)
    packed_own = project(normed_one, space_own, wide)
    mixed_own = attend(packed_own, space_bias, masks, space_blocks)
    mixed_own, space_other = phase(mixed_own, space_other)
    space = [space_own, space_other]
    packed_one = [packed_own, project(normed_one, space[1], wide)]
    mixed_one = [mixed_own, attend(packed_one[1], space_bias, masks, space_blocks)]
    middle = (entered + project_out(mixed_one, space, wide)).astype(bf16)
    middle, time_near = phase(middle, time_near)
    middle = to_places(middle, counts, seq)
    time_far = spread_far(time_near, seq)
    middle, time_far, time_near, ffn_block = phase(middle, time_far, time_near, ffn_block)
    ffn_near = spread_near(ffn_block, seq)
    middle = middle.astype(f32)
    time_own = place(time_block, time_near, time_far, seq, me_array, False)
    time_other = swap(time_own, "tensor", 2, 1)
    normed_two = layer_norm(middle, gains[1], shifts[1])
    packed_own = project(normed_two, time_own, wide)
    mixed_own = attend(packed_own, time_bias, masks, time_blocks)
    mixed_own, time_other = phase(mixed_own, time_other)
    time = [time_own, time_other]
    packed_two = [packed_own, project(normed_two, time[1], wide)]
    mixed_two = [mixed_own, attend(packed_two[1], time_bias, masks, time_blocks)]
    before = middle + project_out(mixed_two, time, wide)
    normed_three = layer_norm(before, gains[2], shifts[2])
    ffn_near, normed_three, before = phase(ffn_near, normed_three, before)
    ffn_far = spread_far(ffn_near, seq)
    ffn_own = place(ffn_block, ffn_near, ffn_far, seq, me_array, False)
    ffn_other = swap(ffn_own, "tensor", 2, 1)
    act_own, du_own, mixed_own, dn_own = ffn(normed_three, cot, ffn_own)
    act_own, ffn_other = phase(act_own, ffn_other)
    act_other, du_other, mixed_other, dn_other = ffn(normed_three, cot, ffn_other)
    mixed = (before + mixed_own + mixed_other).astype(bf16)
    mixed, act_other, du_other, dn_other = phase(mixed, act_other, du_other, dn_other)
    mixed = send_frames(mixed, counts, seq)
    down_other = swap(grad_other([cot], [act_other]), "tensor", 2, 1)
    up_other = grad_other([normed_three], [du_other])
    d_input, gain_three, shift_three = norm_back(before, gains[2], dn_own + dn_other)
    gradient = cot.astype(f32) + d_input
    rounded = gradient.astype(bf16)
    down_other, up_other, rounded = phase(down_other, up_other, rounded)
    up_other = swap(up_other, "tensor", 2, 1)
    down_grads = grad_parts([cot], [act_own], down_other, sizes, me_array)
    down_grads, rounded, up_other = phase(down_grads, rounded, up_other)
    down_state = reduce_far(down_grads, seq)
    upstream = [pull_out(rounded, half, wide) for half in time]
    d_own = attend_back(packed_two[0], upstream[0], time_bias, masks, time_blocks)
    d_own, upstream, down_state, mixed = phase(d_own, upstream, down_state, mixed)
    down_near = near_parts(down_state, seq)
    up_grads = grad_parts([normed_three], [du_own], up_other, sizes, me_array)
    d_other = attend_back(packed_two[1], upstream[1], time_bias, masks, time_blocks)
    d_packed = [d_own, d_other]
    d_input, gain_two, shift_two = norm_back(middle, gains[1], pull_in(d_packed, time, wide))
    rounded_two = (gradient + d_input).astype(bf16)
    rounded_two, d_packed, down_near, up_grads = phase(rounded_two, d_packed, down_near, up_grads)
    rounded_two = join_frames(send_frames(rounded_two, counts, seq), counts, seq)
    left = [normed_two, rounded]
    time_other = grad_other(left, [d_packed[1], mixed_two[1]])
    rounded, time_other, up_grads, mixed, down_near = phase(
        rounded_two, time_other, up_grads, mixed, down_near
    )
    time_other = swap(time_other, "tensor", 2, 1)
    up_state = reduce_far(up_grads, seq)
    time_grads = grad_parts(left, [d_packed[0], mixed_two[0]], time_other, sizes, me_array)
    upstream = [pull_out(rounded, half, wide) for half in space]
    mixed = leave(join_frames(mixed, counts, seq), shapes, seq, me)
    time_grads, upstream, up_state, mixed = phase(time_grads, upstream, up_state, mixed)
    up_near = near_parts(up_state, seq)
    d_other = attend_back(packed_one[1], upstream[1], space_bias, masks, space_blocks)
    left = [normed_one, rounded]
    space_other = grad_other(left, [d_other, mixed_one[1]])
    d_other, up_near, time_grads, space_other, upstream = phase(
        d_other, up_near, time_grads, space_other, upstream
    )
    space_other = swap(space_other, "tensor", 2, 1)
    time_state = reduce_far(time_grads, seq)
    d_own = attend_back(packed_one[0], upstream[0], space_bias, masks, space_blocks)
    space_grads = grad_parts(left, [d_own, mixed_one[0]], space_other, sizes, me_array)
    time_state, space_grads, d_own, d_other, down_near, up_near = phase(
        time_state, space_grads, d_own, d_other, down_near, up_near
    )
    time_near = near_parts(time_state, seq)
    grad_down = reduce_z(down_near)
    grad_up = reduce_z(up_near)
    d_normed = pull_in([d_own, d_other], space, wide)
    d_input, gain_one, shift_one = norm_back(entered, gains[0], d_normed)
    gradient = rounded.astype(f32) + d_input
    time_near, space_grads, gradient = phase(time_near, space_grads, gradient)
    space_state = reduce_far(space_grads, seq)
    grads = leave(gradient.astype(bf16), shapes, seq, me)
    space_state, time_near, gradient = phase(space_state, time_near, gradient)
    space_near = near_parts(space_state, seq)
    grad_time = reduce_z(time_near)
    sums, start = [], 0
    for frame_count, places in counts:
        stop = start + frame_count * places
        sums.append(jnp.sum(gradient[start:stop].reshape(frame_count, places, -1), axis=1))
        start = stop
    grad_table = jnp.dot(onehot.T, jnp.concatenate(sums), precision=highest)
    vector_grads = jnp.concatenate(
        [
            jnp.stack([gain_one, gain_two, gain_three, shift_one, shift_two, shift_three]),
            grad_table,
        ]
    )
    rows = vector_grads.shape[0]
    vector_grads = vector_parts(vector_grads, sizes, rank)
    space_near, vector_grads, grads, grad_down = phase(space_near, vector_grads, grads, grad_down)
    vector_grads = sum_vectors_z(vector_grads, dp)
    vector_grads = sum_vectors_plane(vector_grads, seq, rows)
    grad_space = direct_z(sum_near(space_near, dp, me_array), dp)

    def unpack(member):
        slabs = member[:, :wide].reshape(rows_in, -1, 3, SLAB)
        return slabs.transpose(2, 0, 1, 3).reshape(3, rows_in, -1)

    return (
        *mixed,
        *grads,
        unpack(grad_space),
        grad_space[:, wide:],
        unpack(grad_time.astype(f32)),
        grad_time[:, wide:].astype(f32),
        grad_up.astype(f32),
        grad_down.astype(f32),
        vector_grads[:3],
        vector_grads[3:6],
        vector_grads[6:],
    )


def solution(mesh):
    sizes = (mesh.shape["dp"], mesh.shape["seq"])
    in_specs = (
        P("dp", "seq", "tensor", None),
        P("dp", "seq"),
        P("dp", "seq", "tensor", None),
        P("dp", "seq"),
        P(None, ("dp", "seq"), "tensor"),
        P(("dp", "seq"), "tensor"),
        P(None, ("dp", "seq"), "tensor"),
        P(("dp", "seq"), "tensor"),
        P(("dp", "seq"), "tensor"),
        P(("dp", "seq"), "tensor"),
        P(None, ("dp", "seq", "tensor")),
        P(None, ("dp", "seq", "tensor")),
        P(None, ("dp", "seq", "tensor")),
        P("dp", "seq", "tensor", None),
        P("dp", "seq", "tensor", None),
    )
    out_specs = (
        P("dp", "seq", "tensor", None),
        P("dp", "seq", "tensor", None),
        P("dp", "seq", "tensor", None),
        P("dp", "seq", "tensor", None),
        P(None, ("dp", "seq"), "tensor"),
        P(("dp", "seq"), "tensor"),
        P(None, ("dp", "seq"), "tensor"),
        P(("dp", "seq"), "tensor"),
        P(("dp", "seq"), "tensor"),
        P(("dp", "seq"), "tensor"),
        P(None, ("dp", "seq", "tensor")),
        P(None, ("dp", "seq", "tensor")),
        P(None, ("dp", "seq", "tensor")),
    )
    return jax.shard_map(
        functools.partial(local, sizes),
        mesh=mesh,
        in_specs=in_specs,
        out_specs=out_specs,
        check_vma=False,
    )
```

```python
import functools

import jax
import jax.numpy as jnp
from jax import lax
from jax.experimental import pallas as pl
from jax.experimental.pallas import tpu as pltpu
from jax.sharding import PartitionSpec as P

HDIM = 64
BLOCK = 128

epsilon = 1e-05
masked_score = -1e30
highest = lax.Precision.HIGHEST
bf16 = jnp.bfloat16
f32 = jnp.float32


def swap(operand, axis, size, step):
    return lax.ppermute(operand, axis, [(i, i ^ step) for i in range(size)])


def norm_stats(operand):
    centred = operand - jnp.mean(operand, axis=-1, keepdims=True)
    inverse = lax.rsqrt(jnp.mean(centred * centred, axis=-1, keepdims=True) + epsilon)
    return centred * inverse, inverse


def layer_norm(operand, gain_row, shift_row):
    standard, _ = norm_stats(operand)
    return (standard * gain_row + shift_row).astype(bf16)


def norm_back(operand, gain_row, upstream):
    standard, inverse = norm_stats(operand)
    scaled = upstream * gain_row
    inner = (
        scaled
        - jnp.mean(scaled, axis=-1, keepdims=True)
        - standard * jnp.mean(scaled * standard, axis=-1, keepdims=True)
    )
    return inverse * inner, jnp.sum(upstream * standard, axis=0), jnp.sum(upstream, axis=0)


SLAB = 2 * HDIM


def small_cost():
    return pl.CostEstimate(flops=1024, bytes_accessed=1024, transcendentals=0)


def nt(left, right):
    return lax.dot_general(left, right, (((1,), (1,)), ((), ())), preferred_element_type=f32)


def nn(left, right):
    return lax.dot_general(left, right, (((1,), (0,)), ((), ())), preferred_element_type=f32)


def tn(left, right):
    return lax.dot_general(left, right, (((0,), (0,)), ((), ())), preferred_element_type=f32)


def soft_weights(scores):
    shifted = jnp.exp(scores - jnp.max(scores, axis=-1, keepdims=True))
    return shifted * (1.0 / jnp.sum(shifted, axis=-1, keepdims=True))


def attend_kernel(blocks, bias_ref, mask_ref, p_ref, o_ref):
    items = [(start, size, masked, head) for start, size, masked in blocks for head in (0, 1)]
    scores = []
    for start, size, masked, head in items:
        rows = pl.ds(start, size)
        part = nt(p_ref[rows, :SLAB] * mask_ref[head, :size, :], p_ref[rows, SLAB : 2 * SLAB])
        scores.append(part + bias_ref[...] if masked else part)
    weights = [soft_weights(part).astype(bf16) for part in scores]
    parts = [
        nn(part, p_ref[pl.ds(start, size), 2 * SLAB :] * mask_ref[2 + head, :size, :])
        for part, (start, size, _, head) in zip(weights, items)
    ]
    for at, (start, size, _) in enumerate(blocks):
        o_ref[pl.ds(start, size), :] = (parts[2 * at] + parts[2 * at + 1]).astype(bf16)


def attend_back_kernel(blocks, bias_ref, mask_ref, p_ref, d_ref, o_ref):
    items = [(start, size, masked, head) for start, size, masked in blocks for head in (0, 1)]
    scores, d_weights = [], []
    for start, size, masked, head in items:
        rows = pl.ds(start, size)
        part = nt(p_ref[rows, :SLAB] * mask_ref[head, :size, :], p_ref[rows, SLAB : 2 * SLAB])
        scores.append(part + bias_ref[...] if masked else part)
        d_weights.append(nt(d_ref[rows, :] * mask_ref[2 + head, :size, :], p_ref[rows, 2 * SLAB :]))
    weights = [soft_weights(part) for part in scores]
    d_scores = [
        (part * (grad - jnp.sum(part * grad, axis=-1, keepdims=True))).astype(bf16)
        for part, grad in zip(weights, d_weights)
    ]
    weights = [part.astype(bf16) for part in weights]
    for index, (start, size, _) in enumerate(blocks):
        rows = pl.ds(start, size)
        dq, dk, dv = 0.0, 0.0, 0.0
        for head in (0, 1):
            scaled, whole = mask_ref[head, :size, :], mask_ref[2 + head, :size, :]
            d_score, weight = d_scores[2 * index + head], weights[2 * index + head]
            dq += nn(d_score, p_ref[rows, SLAB : 2 * SLAB] * scaled)
            dk += tn(d_score, p_ref[rows, :SLAB] * scaled)
            dv += tn(weight, d_ref[rows, :] * whole)
        o_ref[rows, :SLAB] = dq.astype(bf16)
        o_ref[rows, SLAB : 2 * SLAB] = dk.astype(bf16)
        o_ref[rows, 2 * SLAB :] = dv.astype(bf16)


def head_masks(rows):
    low = lax.broadcasted_iota(jnp.int32, (rows, SLAB), 1) < HDIM
    masks = jnp.stack([low, ~low]).astype(bf16)
    return jnp.concatenate([masks * (HDIM**-0.5), masks])


def slab_spec(count, width):
    return pl.BlockSpec((count, width), lambda i: (0, i))


def attend_specs(packed, bias, masks, blocks, products):
    count, width = packed.shape
    slabs = width // (3 * SLAB)
    specs = [
        pl.BlockSpec(bias.shape, lambda i: (0, 0)),
        pl.BlockSpec(masks.shape, lambda i: (0, 0, 0)),
        slab_spec(count, 3 * SLAB),
    ]
    scores = 2 * slabs * sum(size * size for _, size, _ in blocks)
    cost = pl.CostEstimate(
        flops=2 * products * scores * SLAB,
        bytes_accessed=count * width * products,
        transcendentals=scores,
    )
    return count, slabs, specs, cost


def attend(packed, bias, masks, blocks):
    count, slabs, specs, cost = attend_specs(packed, bias, masks, blocks, 2)
    return pl.pallas_call(
        functools.partial(attend_kernel, blocks),
        out_shape=jax.ShapeDtypeStruct((count, slabs * SLAB), bf16),
        grid=(slabs,),
        in_specs=specs,
        out_specs=slab_spec(count, SLAB),
        cost_estimate=cost,
        compiler_params=pltpu.CompilerParams(vmem_limit_bytes=32 * 2**20),
    )(bias, masks, packed)


def attend_back(packed, upstream, bias, masks, blocks):
    count, slabs, specs, cost = attend_specs(packed, bias, masks, blocks, 5)
    return pl.pallas_call(
        functools.partial(attend_back_kernel, blocks),
        out_shape=jax.ShapeDtypeStruct(packed.shape, bf16),
        grid=(slabs,),
        in_specs=[*specs, slab_spec(count, SLAB)],
        out_specs=slab_spec(count, 3 * SLAB),
        cost_estimate=cost,
        compiler_params=pltpu.CompilerParams(vmem_limit_bytes=32 * 2**20),
    )(bias, masks, packed, upstream)


def place_kernel(order, count, relative, me_ref, *refs):
    pieces, out_ref = refs[:count], refs[count]
    for piece, row, kz, ks in order:
        at_z = jnp.bitwise_xor(me_ref[0], kz) if relative else kz
        at = at_z, jnp.bitwise_xor(me_ref[1], ks)
        out_ref[at] = pieces[piece][row]


def phase(*state):
    return lax.optimization_barrier(state)


def double_z(state, step, dp):
    return jnp.concatenate([state, swap(state, "dp", dp, step)])


def parts_z(shard, dp):
    return [shard] + [swap(shard, "dp", dp, k) for k in range(1, dp)]


def spread_z(state, step, dp):
    while step < dp:
        state = double_z(state, step, dp)
        step *= 2
    return state


def spread_near(block, seq):
    if seq == 4:
        return [swap(block, "seq", seq, 1), swap(block, "seq", seq, 2)]
    return [swap(block, "seq", seq, step) for step in range(1, seq)]


def spread_far(near, seq):
    if seq != 4:
        return []
    from_x, from_y = near
    half = from_x.shape[0] // 2
    return [swap(from_y[:half], "seq", seq, 1), swap(from_x[half:], "seq", seq, 2)]


def place(block, near, far, seq, me, relative=True):
    dp, rows, width = block.shape
    half = dp // 2
    pieces = [block, *near, *far]
    order = [(index, k, k, index) for index in range(1 + len(near)) for k in range(dp)]
    if far:
        order += [(3, k, k, 3) for k in range(half)]
        order += [(4, k - half, k, 3) for k in range(half, dp)]
    whole = pl.pallas_call(
        functools.partial(place_kernel, order, len(pieces), relative),
        out_shape=jax.ShapeDtypeStruct((dp, seq, rows, width), block.dtype),
        grid=(width // COLUMNS,),
        in_specs=[pl.BlockSpec(memory_space=pltpu.SMEM)]
        + [
            pl.BlockSpec((piece.shape[0], rows, COLUMNS), lambda i: (0, 0, i)) for piece in pieces
        ],
        out_specs=pl.BlockSpec((dp, seq, rows, COLUMNS), lambda i: (0, 0, 0, i)),
        cost_estimate=pl.CostEstimate(
            flops=0, bytes_accessed=4 * dp * seq * rows * width, transcendentals=0
        ),
        compiler_params=pltpu.CompilerParams(vmem_limit_bytes=32 * 2**20),
    )(me, *pieces)
    return whole.reshape(dp * seq * rows, width)


def each_block(pairs, splits, left, right, store):
    at = pl.program_id(0)
    if pairs == 1:
        store(tn(left[0][...], right[0][...]))
        return
    for pair in range(pairs):

        @pl.when((at >= splits[pair]) & (at < splits[pair + 1]))
        def _():
            store(tn(left[pair][...], right[pair][...]))


def grad_kernel(pairs, splits, *refs):
    left, right, out_ref = refs[:pairs], refs[pairs : 2 * pairs], refs[-1]

    def store(total):
        out_ref[...] = total.astype(bf16)

    each_block(pairs, splits, left, right, store)


def grad_parts_kernel(pairs, splits, dp, seq, me_ref, *refs):
    left, right, other_ref = refs[:pairs], refs[pairs : 2 * pairs], refs[2 * pairs]
    outs, held = refs[2 * pairs + 1 : -1], refs[-1]
    rows = other_ref.shape[0] // (dp * seq)

    def store(total):
        total = total + other_ref[...].astype(f32)
        held[...] = total.astype(bf16).reshape(held.shape)

    each_block(pairs, splits, left, right, store)
    for k in range(seq):
        owner = jnp.bitwise_xor(me_ref[1], k)
        for z in range(dp):
            part = held[z * seq + owner]
            if seq == 4 and k == 3:
                outs[3 + z // (dp // 2)][z % (dp // 2)] = part
            else:
                outs[k][z] = part


COLUMNS = 512


def grad_specs(left, right):
    rows, features = left[0].shape
    splits = [0]
    for member in right:
        splits.append(splits[-1] + member.shape[1] // COLUMNS)
    specs = [pl.BlockSpec(member.shape, lambda i: (0, 0)) for member in left]

    def columns(first, last):
        return lambda i: (0, jnp.clip(i - first, 0, last - first - 1))

    for first, last in zip(splits, splits[1:]):
        specs.append(pl.BlockSpec((rows, COLUMNS), columns(first, last)))
    width = splits[-1] * COLUMNS
    cost = pl.CostEstimate(
        flops=2 * rows * features * width,
        bytes_accessed=4 * width * features,
        transcendentals=0,
    )
    return splits, specs, width, cost


def grad_other(left, right):
    splits, specs, width, cost = grad_specs(left, right)
    features = left[0].shape[1]
    return pl.pallas_call(
        functools.partial(grad_kernel, len(left), splits),
        out_shape=jax.ShapeDtypeStruct((features, width), bf16),
        grid=(width // COLUMNS,),
        in_specs=specs,
        out_specs=pl.BlockSpec((features, COLUMNS), lambda i: (0, i)),
        cost_estimate=small_cost(),
        compiler_params=pltpu.CompilerParams(vmem_limit_bytes=32 * 2**20),
    )(*left, *right)


def grad_parts(left, right, other, sizes, me):
    dp, seq = sizes
    splits, specs, width, cost = grad_specs(left, right)
    features = left[0].shape[1]
    rows = features // (dp * seq)
    depths = [dp] * seq if seq != 4 else [dp, dp, dp, dp // 2, dp - dp // 2]
    return pl.pallas_call(
        functools.partial(grad_parts_kernel, len(left), splits, dp, seq),
        out_shape=[jax.ShapeDtypeStruct((depth, rows, width), bf16) for depth in depths],
        grid=(width // COLUMNS,),
        in_specs=[
            pl.BlockSpec(memory_space=pltpu.SMEM),
            *specs,
            pl.BlockSpec((features, COLUMNS), lambda i: (0, i)),
        ],
        out_specs=[pl.BlockSpec((depth, rows, COLUMNS), lambda i: (0, 0, i)) for depth in depths],
        scratch_shapes=[pltpu.VMEM((dp * seq, rows, COLUMNS), bf16)],
        cost_estimate=cost,
        compiler_params=pltpu.CompilerParams(vmem_limit_bytes=40 * 2**20),
    )(me, *left, *right, other)


def reduce_far(parts, seq):
    if seq != 4:
        return parts[0], parts[1:]
    own, to_x, to_y, low, high = parts
    half = low.shape[0]
    from_x, from_y = swap(low, "seq", seq, 1), swap(high, "seq", seq, 2)
    to_x = jnp.concatenate([to_x[:half], to_x[half:] + from_y])
    to_y = jnp.concatenate([to_y[:half] + from_x, to_y[half:]])
    return own, [to_x, to_y]


def sum_kernel(count, dp, me_ref, *refs):
    parts, outs, held = refs[:count], refs[count:-1], refs[-1]
    held[...] = sum(part[...].astype(f32) for part in parts).astype(bf16)
    half = dp // 2
    for k in range(dp):
        outs[k // half][k % half] = held[jnp.bitwise_xor(me_ref[0], k)]


def near_parts(state, seq):
    own, sends = state
    return [own] + [swap(part, "seq", seq, 1 + step) for step, part in enumerate(sends)]


def sum_near(parts, dp, me):
    rows, width = parts[0].shape[1:]
    spec = pl.BlockSpec((dp, rows, COLUMNS), lambda i: (0, 0, i))
    out = pl.BlockSpec((dp // 2, rows, COLUMNS), lambda i: (0, 0, i))
    return pl.pallas_call(
        functools.partial(sum_kernel, len(parts), dp),
        out_shape=[jax.ShapeDtypeStruct((dp // 2, rows, width), bf16)] * 2,
        grid=(width // COLUMNS,),
        in_specs=[pl.BlockSpec(memory_space=pltpu.SMEM)] + [spec] * len(parts),
        out_specs=[out, out],
        scratch_shapes=[pltpu.VMEM((dp, rows, COLUMNS), bf16)],
        cost_estimate=pl.CostEstimate(
            flops=0, bytes_accessed=2 * (len(parts) + 1) * dp * rows * width, transcendentals=0
        ),
        compiler_params=pltpu.CompilerParams(vmem_limit_bytes=32 * 2**20),
    )(me, *parts)


def reduce_z(parts):
    total = sum(part.astype(f32) for part in parts).astype(bf16)
    return lax.psum_scatter(total, "dp", scatter_dimension=0)


def direct_z(state, dp):
    keep, send = state
    half = dp // 2
    rows = [keep[k] for k in range(half)] + [send[k] for k in range(half)]
    return sum(
        [rows[0].astype(f32)] + [swap(rows[k], "dp", dp, k).astype(f32) for k in range(1, dp)]
    )


def xor_onehot(count, rank):
    index = lax.broadcasted_iota(jnp.int32, (count, count), 0)
    other = lax.broadcasted_iota(jnp.int32, (count, count), 1)
    return (jnp.bitwise_xor(index, rank) == other).astype(f32)


def vectors_plane(shard, seq):
    found = jnp.stack([shard, swap(shard, "tensor", 2, 1)])
    return jnp.stack([found] + [swap(found, "seq", seq, k) for k in range(1, seq)])


def vectors_z(found, dp, rank):
    found = jnp.stack([found] + [swap(found, "dp", dp, k) for k in range(1, dp)])
    rows, width = found.shape[-2:]
    count = found.size // (rows * width)
    found = found.reshape(count, rows * width).astype(f32)
    placed = jnp.dot(xor_onehot(count, rank), found, precision=highest)
    return placed.reshape(count, rows, width).transpose(1, 0, 2).reshape(rows, count * width)


def vector_parts(whole, sizes, rank):
    dp, seq = sizes
    rows, features = whole.shape
    count = dp * seq * 2
    width = features // count
    parts = whole.reshape(rows, count, width).transpose(1, 0, 2).reshape(count, rows * width)
    parts = jnp.dot(xor_onehot(count, rank), parts, precision=highest)
    return parts.reshape(dp, seq, 2, rows * width)


def sum_vectors_z(parts, dp):
    total = parts[0]
    for step in range(1, dp):
        total = total + swap(parts[step], "dp", dp, step)
    return total


def sum_vectors_plane(parts, seq, rows):
    total = parts[0]
    for step in range(1, seq):
        total = total + swap(parts[step], "seq", seq, step)
    total = total[0] + swap(total[1], "tensor", 2, 1)
    return total.reshape(rows, -1)


def turn(operand, axis, size, rank):
    bit = 1
    shape = operand.shape
    while bit < size:
        split = operand.reshape(shape[:axis] + (size // (2 * bit), 2, bit) + shape[axis + 1 :])
        low, high = [lax.index_in_dim(split, at, axis + 1, keepdims=False) for at in (0, 1)]
        moved = jnp.bitwise_and(rank, bit) != 0
        both = [jnp.where(moved, high, low), jnp.where(moved, low, high)]
        operand = jnp.stack(both, axis=axis + 1).reshape(shape)
        bit *= 2
    return operand


def enter(first, second, seq, me):
    s, t = me[1], me[2]
    shapes = [member.shape for member in (first, second)]

    def pick(which):
        return jnp.concatenate(
            [
                lax.dynamic_index_in_dim(member, which, 0, keepdims=False).reshape(-1, shape[3])
                for member, shape in zip((first, second), shapes)
            ]
        )

    own, received = pick(t), swap(pick(1 - t), "tensor", 2, 1)
    rows, start = [], 0
    for shape in shapes:
        frames, places, features = shape[1:]
        stop = start + frames * places
        halves = [
            member[start:stop].reshape(frames, places, features) for member in (own, received)
        ]
        both = jnp.concatenate(halves, axis=1).reshape(frames, seq, -1, features)
        rows.append(turn(both, 1, seq, s).reshape(-1, features))
        start = stop
    return jnp.concatenate(rows)


def leave(tokens, shapes, seq, me):
    s, t = me[1], me[2]
    features = tokens.shape[1]
    own, other, start = [], [], 0
    for shape in shapes:
        frames, places = shape[1:3]
        stop = start + 2 * frames * places
        member = turn(tokens[start:stop].reshape(frames, seq, -1, features), 1, seq, s)
        member = member.reshape(frames, 2, places, features)
        own.append(member[:, 0].reshape(-1, features))
        other.append(member[:, 1].reshape(-1, features))
        start = stop
    own, received = jnp.concatenate(own), swap(jnp.concatenate(other), "tensor", 2, 1)
    results, start = [], 0
    for shape in shapes:
        frames, places = shape[1:3]
        stop = start + frames * places
        mine, theirs = own[start:stop], received[start:stop]
        both = jnp.stack([jnp.where(t == 0, mine, theirs), jnp.where(t == 0, theirs, mine)])
        results.append(both.reshape(shape))
        start = stop
    return results


def to_places(tokens, counts, seq):
    features = tokens.shape[1]
    members, start = [], 0
    for frames, places in counts:
        stop = start + frames * places
        members.append(tokens[start:stop].reshape(frames, seq, places // seq, features))
        start = stop
    pieces = [
        jnp.concatenate([member[:, step].reshape(-1, features) for member in members])
        for step in range(seq)
    ]
    pieces = jnp.stack(
        [pieces[0]] + [swap(pieces[step], "seq", seq, step) for step in range(1, seq)]
    )
    rows, start = [], 0
    for frames, places in counts:
        local = places // seq
        group = BLOCK // (frames * seq)
        stop = start + frames * local
        member = pieces[:, start:stop].reshape(seq, frames, local // group, group, features)
        rows.append(member.transpose(2, 0, 1, 3, 4).reshape(-1, features))
        start = stop
    return jnp.concatenate(rows)


def send_frames(tokens, counts, seq):
    features = tokens.shape[1]
    members, start = [], 0
    for frames, places in counts:
        local = places // seq
        group = BLOCK // (frames * seq)
        stop = start + seq * frames * local
        member = tokens[start:stop].reshape(local // group, seq, frames, group, features)
        members.append(member.transpose(1, 2, 0, 3, 4).reshape(seq, -1, features))
        start = stop
    pieces = jnp.concatenate(members, axis=1)
    return [pieces[0]] + [swap(pieces[step], "seq", seq, step) for step in range(1, seq)]


def join_frames(pieces, counts, seq):
    pieces = jnp.stack(pieces)
    features = pieces.shape[-1]
    rows, start = [], 0
    for frames, places in counts:
        local = places // seq
        stop = start + frames * local
        member = pieces[:, start:stop].reshape(seq, frames, local, features)
        rows.append(member.transpose(1, 0, 2, 3).reshape(-1, features))
        start = stop
    return jnp.concatenate(rows)


def allowed_bias(allowed):
    return jnp.where(allowed, 0.0, masked_score).astype(f32)


ROOT = 0.7978845608028654
CUBE = 0.044715


def ffn_kernel(n_ref, c_ref, up_ref, down_ref, z_ref, du_ref, mixed_ref, dn_ref):
    @pl.when(pl.program_id(0) == 0)
    def _():
        mixed_ref[...] = jnp.zeros_like(mixed_ref)
        dn_ref[...] = jnp.zeros_like(dn_ref)

    u = nn(n_ref[...], up_ref[...])
    da = nn(c_ref[...], down_ref[...])
    square = u * u
    bent = jnp.tanh(u * (ROOT + ROOT * CUBE * square))
    half = 0.5 + 0.5 * bent
    z = (u * half).astype(bf16)
    slope = half + (0.5 * u) * (1.0 - bent * bent) * (ROOT + 3.0 * ROOT * CUBE * square)
    du = (da * slope).astype(bf16)
    z_ref[...] = z
    du_ref[...] = du
    mixed_ref[...] += nt(z, down_ref[...])
    dn_ref[...] += nt(du, up_ref[...])


def ffn(normed, cotangent, pack):
    count, features = normed.shape
    hidden = pack.shape[1] // 2
    steps = hidden // COLUMNS
    rows = pl.BlockSpec((count, features), lambda i: (0, 0))
    units = pl.BlockSpec((count, COLUMNS), lambda i: (0, i))
    return pl.pallas_call(
        ffn_kernel,
        out_shape=[jax.ShapeDtypeStruct((count, hidden), bf16)] * 2
        + [jax.ShapeDtypeStruct((count, features), f32)] * 2,
        grid=(steps,),
        in_specs=[
            rows,
            rows,
            pl.BlockSpec((features, COLUMNS), lambda i: (0, i)),
            pl.BlockSpec((features, COLUMNS), lambda i: (0, i + steps)),
        ],
        out_specs=[units, units, rows, rows],
        cost_estimate=pl.CostEstimate(
            flops=8 * count * features * hidden,
            bytes_accessed=4 * features * hidden,
            transcendentals=count * hidden,
        ),
        compiler_params=pltpu.CompilerParams(vmem_limit_bytes=48 * 2**20),
    )(normed, cotangent, pack, pack)


def project(rows, half, stop):
    return jnp.dot(rows, half[:, :stop], preferred_element_type=f32).astype(bf16)


def project_out(mixed, halves, start):
    return sum(nt(member, half[:, start:]) for member, half in zip(mixed, halves))


def pull_out(gradient, half, start):
    return jnp.dot(gradient, half[:, start:], preferred_element_type=f32).astype(bf16)


def pull_in_kernel(own_ref, other_ref, own_half_ref, other_half_ref, o_ref):
    o_ref[...] = nt(own_ref[...], own_half_ref[...]) + nt(other_ref[...], other_half_ref[...])


def pull_in(packed, halves, stop):
    count = packed[0].shape[0]
    features = halves[0].shape[0]
    columns_of = 2 * SLAB
    rows = pl.BlockSpec((count, stop), lambda i: (0, 0))
    half = pl.BlockSpec((columns_of, stop), lambda i: (i, 0))
    return pl.pallas_call(
        pull_in_kernel,
        out_shape=jax.ShapeDtypeStruct((count, features), f32),
        grid=(features // columns_of,),
        in_specs=[rows, rows, half, half],
        out_specs=pl.BlockSpec((count, columns_of), lambda i: (0, i)),
        cost_estimate=small_cost(),
        compiler_params=pltpu.CompilerParams(vmem_limit_bytes=32 * 2**20),
    )(*packed, *halves)


def local(
    sizes,
    clips_a,
    actions_a,
    clips_b,
    actions_b,
    space_in,
    space_out,
    time_in,
    time_out,
    ffn_up,
    ffn_down,
    norm_gain,
    norm_shift,
    action_table,
    cot_a,
    cot_b,
):
    dp, seq = sizes
    me = [lax.axis_index(name) for name in ("dp", "seq", "tensor")]
    rank = (me[0] * seq + me[1]) * 2 + me[2]
    me_array = jnp.stack(me).astype(jnp.int32)
    rows_in, wide = space_in.shape[1], 3 * space_in.shape[2]

    def pack(inward, outward):
        slabs = inward.reshape(3, rows_in, -1, SLAB).transpose(1, 2, 0, 3)
        return jnp.concatenate([slabs.reshape(rows_in, wide), outward], axis=1)

    shapes = [clips_a.shape, clips_b.shape]
    frames = clips_a.shape[1]
    counts = [(shape[1], 2 * shape[2]) for shape in shapes]

    space_block = lax.all_gather(pack(space_in, space_out), "dp", axis=0)
    vectors = vectors_plane(jnp.concatenate([norm_gain, norm_shift, action_table]), seq)
    cot = to_places(enter(cot_a, cot_b, seq, me), counts, seq)
    clips = enter(clips_a, clips_b, seq, me)
    time_shard = pack(time_in, time_out)[None]
    ffn_shard = jnp.concatenate([ffn_up, ffn_down], axis=1)
    space_block, vectors, clips, cot, time_shard, ffn_shard = phase(
        space_block, vectors, clips, cot, time_shard, ffn_shard
    )
    vectors = vectors_z(vectors, dp, rank)
    space_near = spread_near(space_block, seq)
    time_block = lax.all_gather(time_shard[0], "dp", axis=0)

    gains, shifts, table = vectors[:3], vectors[3:6], vectors[6:]
    acts = jnp.concatenate(
        [
            lax.dynamic_index_in_dim(member, me[2], 0, keepdims=False)
            for member in (actions_a, actions_b)
        ]
    )
    onehot = (
        acts[:, None] == lax.broadcasted_iota(jnp.int32, (1, table.shape[0]), 1)
    ).astype(f32)
    rows_of = jnp.dot(onehot, table, precision=highest)
    spread = jnp.concatenate(
        [
            jnp.broadcast_to(
                rows_of[index * frames : (index + 1) * frames, None, :],
                (frames, places, table.shape[1]),
            ).reshape(-1, table.shape[1])
            for index, (_, places) in enumerate(counts)
        ]
    )
    entered = clips.astype(f32) + spread

    places_a, places_b = counts[0][1], counts[1][1]
    space_blocks = [(frame * places_a, places_a, False) for frame in range(frames)]
    space_blocks.append((frames * places_a, frames * places_b, True))
    index = lax.broadcasted_iota(jnp.int32, (frames * places_b, 1), 0) // places_b
    space_bias = allowed_bias(index == index.reshape(1, -1))
    total_tokens = clips.shape[0]
    time_blocks = [(start, BLOCK, True) for start in range(0, total_tokens, BLOCK)]
    group = BLOCK // (frames * seq)
    token = lax.broadcasted_iota(jnp.int32, (BLOCK, 1), 0)
    spot = token % group
    frame_id = (
        jnp.bitwise_xor(token // (frames * group), me[1]) * frames + (token // group) % frames
    )
    time_bias = allowed_bias(
        (spot == spot.reshape(1, -1)) & (frame_id.reshape(1, -1) <= frame_id)
    )

    masks = head_masks(max(BLOCK, places_a))

    normed_one = layer_norm(entered, gains[0], shifts[0])
    space_near, normed_one, entered = phase(space_near, normed_one, entered)
    space_far = spread_far(space_near, seq)
    space_far, space_near, time_block, ffn_shard = phase(
        space_far, space_near, time_block, ffn_shard
    )
    ffn_block = lax.all_gather(ffn_shard, "dp", axis=0)
    time_near = spread_near(time_block, seq)
    space_own = place(space_block, space_near, space_far, seq, me_array, False)
    space_other = swap(space_own, "tensor", 2, 1)
    packed_own = project(normed_one, space_own, wide)
    mixed_own = attend(packed_own, space_bias, masks, space_blocks)
    mixed_own, space_other = phase(mixed_own, space_other)
    space = [space_own, space_other]
    packed_one = [packed_own, project(normed_one, space[1], wide)]
    mixed_one = [mixed_own, attend(packed_one[1], space_bias, masks, space_blocks)]
    middle = (entered + project_out(mixed_one, space, wide)).astype(bf16)
    middle, time_near = phase(middle, time_near)
    middle = to_places(middle, counts, seq)
    time_far = spread_far(time_near, seq)
    middle, time_far, time_near, ffn_block = phase(middle, time_far, time_near, ffn_block)
    ffn_near = spread_near(ffn_block, seq)
    middle = middle.astype(f32)
    time_own = place(time_block, time_near, time_far, seq, me_array, False)
    time_other = swap(time_own, "tensor", 2, 1)
    normed_two = layer_norm(middle, gains[1], shifts[1])
    packed_own = project(normed_two, time_own, wide)
    mixed_own = attend(packed_own, time_bias, masks, time_blocks)
    mixed_own, time_other = phase(mixed_own, time_other)
    time = [time_own, time_other]
    packed_two = [packed_own, project(normed_two, time[1], wide)]
    mixed_two = [mixed_own, attend(packed_two[1], time_bias, masks, time_blocks)]
    before = middle + project_out(mixed_two, time, wide)
    normed_three = layer_norm(before, gains[2], shifts[2])
    ffn_near, normed_three, before = phase(ffn_near, normed_three, before)
    ffn_far = spread_far(ffn_near, seq)
    ffn_own = place(ffn_block, ffn_near, ffn_far, seq, me_array, False)
    ffn_other = swap(ffn_own, "tensor", 2, 1)
    act_own, du_own, mixed_own, dn_own = ffn(normed_three, cot, ffn_own)
    act_own, ffn_other = phase(act_own, ffn_other)
    act_other, du_other, mixed_other, dn_other = ffn(normed_three, cot, ffn_other)
    mixed = (before + mixed_own + mixed_other).astype(bf16)
    mixed, act_other, du_other, dn_other = phase(mixed, act_other, du_other, dn_other)
    mixed = send_frames(mixed, counts, seq)
    down_other = swap(grad_other([cot], [act_other]), "tensor", 2, 1)
    up_other = grad_other([normed_three], [du_other])
    d_input, gain_three, shift_three = norm_back(before, gains[2], dn_own + dn_other)
    gradient = cot.astype(f32) + d_input
    rounded = gradient.astype(bf16)
    down_other, up_other, rounded = phase(down_other, up_other, rounded)
    up_other = swap(up_other, "tensor", 2, 1)
    down_grads = grad_parts([cot], [act_own], down_other, sizes, me_array)
    down_grads, rounded, up_other = phase(down_grads, rounded, up_other)
    down_state = reduce_far(down_grads, seq)
    upstream = [pull_out(rounded, half, wide) for half in time]
    d_own = attend_back(packed_two[0], upstream[0], time_bias, masks, time_blocks)
    d_own, upstream, down_state, mixed = phase(d_own, upstream, down_state, mixed)
    down_near = near_parts(down_state, seq)
    up_grads = grad_parts([normed_three], [du_own], up_other, sizes, me_array)
    d_other = attend_back(packed_two[1], upstream[1], time_bias, masks, time_blocks)
    d_packed = [d_own, d_other]
    d_input, gain_two, shift_two = norm_back(middle, gains[1], pull_in(d_packed, time, wide))
    rounded_two = (gradient + d_input).astype(bf16)
    rounded_two, d_packed, down_near, up_grads = phase(rounded_two, d_packed, down_near, up_grads)
    rounded_two = join_frames(send_frames(rounded_two, counts, seq), counts, seq)
    left = [normed_two, rounded]
    time_other = grad_other(left, [d_packed[1], mixed_two[1]])
    rounded, time_other, up_grads, mixed, down_near = phase(
        rounded_two, time_other, up_grads, mixed, down_near
    )
    time_other = swap(time_other, "tensor", 2, 1)
    up_state = reduce_far(up_grads, seq)
    time_grads = grad_parts(left, [d_packed[0], mixed_two[0]], time_other, sizes, me_array)
    upstream = [pull_out(rounded, half, wide) for half in space]
    mixed = leave(join_frames(mixed, counts, seq), shapes, seq, me)
    time_grads, upstream, up_state, mixed = phase(time_grads, upstream, up_state, mixed)
    up_near = near_parts(up_state, seq)
    d_other = attend_back(packed_one[1], upstream[1], space_bias, masks, space_blocks)
    left = [normed_one, rounded]
    space_other = grad_other(left, [d_other, mixed_one[1]])
    d_other, up_near, time_grads, space_other, upstream = phase(
        d_other, up_near, time_grads, space_other, upstream
    )
    space_other = swap(space_other, "tensor", 2, 1)
    time_state = reduce_far(time_grads, seq)
    d_own = attend_back(packed_one[0], upstream[0], space_bias, masks, space_blocks)
    time_state, space_other, d_own, d_other, down_near, up_near = phase(
        time_state, space_other, d_own, d_other, down_near, up_near
    )
    time_near = near_parts(time_state, seq)
    space_grads = grad_parts(left, [d_own, mixed_one[0]], space_other, sizes, me_array)
    grad_down = reduce_z(down_near)
    grad_up = reduce_z(up_near)
    d_normed = pull_in([d_own, d_other], space, wide)
    d_input, gain_one, shift_one = norm_back(entered, gains[0], d_normed)
    gradient = rounded.astype(f32) + d_input
    time_near, space_grads, gradient = phase(time_near, space_grads, gradient)
    space_state = reduce_far(space_grads, seq)
    space_state, time_near, gradient = phase(space_state, time_near, gradient)
    grads = leave(gradient.astype(bf16), shapes, seq, me)
    space_near = near_parts(space_state, seq)
    grad_time = reduce_z(time_near)
    sums, start = [], 0
    for frame_count, places in counts:
        stop = start + frame_count * places
        sums.append(jnp.sum(gradient[start:stop].reshape(frame_count, places, -1), axis=1))
        start = stop
    grad_table = jnp.dot(onehot.T, jnp.concatenate(sums), precision=highest)
    vector_grads = jnp.concatenate(
        [
            jnp.stack([gain_one, gain_two, gain_three, shift_one, shift_two, shift_three]),
            grad_table,
        ]
    )
    rows = vector_grads.shape[0]
    vector_grads = vector_parts(vector_grads, sizes, rank)
    space_near, vector_grads, grads, grad_down = phase(space_near, vector_grads, grads, grad_down)
    vector_grads = sum_vectors_z(vector_grads, dp)
    vector_grads = sum_vectors_plane(vector_grads, seq, rows)
    grad_space = direct_z(sum_near(space_near, dp, me_array), dp)

    def unpack(member):
        slabs = member[:, :wide].reshape(rows_in, -1, 3, SLAB)
        return slabs.transpose(2, 0, 1, 3).reshape(3, rows_in, -1)

    return (
        *mixed,
        *grads,
        unpack(grad_space),
        grad_space[:, wide:],
        unpack(grad_time.astype(f32)),
        grad_time[:, wide:].astype(f32),
        grad_up.astype(f32),
        grad_down.astype(f32),
        vector_grads[:3],
        vector_grads[3:6],
        vector_grads[6:],
    )


def solution(mesh):
    sizes = (mesh.shape["dp"], mesh.shape["seq"])
    in_specs = (
        P("dp", "seq", "tensor", None),
        P("dp", "seq"),
        P("dp", "seq", "tensor", None),
        P("dp", "seq"),
        P(None, ("dp", "seq"), "tensor"),
        P(("dp", "seq"), "tensor"),
        P(None, ("dp", "seq"), "tensor"),
        P(("dp", "seq"), "tensor"),
        P(("dp", "seq"), "tensor"),
        P(("dp", "seq"), "tensor"),
        P(None, ("dp", "seq", "tensor")),
        P(None, ("dp", "seq", "tensor")),
        P(None, ("dp", "seq", "tensor")),
        P("dp", "seq", "tensor", None),
        P("dp", "seq", "tensor", None),
    )
    out_specs = (
        P("dp", "seq", "tensor", None),
        P("dp", "seq", "tensor", None),
        P("dp", "seq", "tensor", None),
        P("dp", "seq", "tensor", None),
        P(None, ("dp", "seq"), "tensor"),
        P(("dp", "seq"), "tensor"),
        P(None, ("dp", "seq"), "tensor"),
        P(("dp", "seq"), "tensor"),
        P(("dp", "seq"), "tensor"),
        P(("dp", "seq"), "tensor"),
        P(None, ("dp", "seq", "tensor")),
        P(None, ("dp", "seq", "tensor")),
        P(None, ("dp", "seq", "tensor")),
    )
    return jax.shard_map(
        functools.partial(local, sizes),
        mesh=mesh,
        in_specs=in_specs,
        out_specs=out_specs,
        check_vma=False,
    )
```
